256 devices in a mesh: tm: 8 (over z_lo, y), space: 32 (over x, z_hi, core).
Axes of the slice: x: 4, y: 4, z: 8 (z_hi: 4, z_lo: 2; z = z_hi * 2 + z_lo), core: 2. Of those that a mesh axis runs over, the one named last changes fastest.
Arguments:
- video: bfloat16 [32, 256, 128, 128], P('tm', 'space'), may hold values from -10 to 10
- gain_first: float32 [128], replicated, may hold values from 0.1 to 1.9
- spatial_first: bfloat16 [9, 128, 128], replicated, may hold values from -0.1875 to 0.1875
- temporal_first: bfloat16 [3, 128, 128], replicated, may hold values from -0.3125 to 0.3125
- gain_second: float32 [128], replicated, may hold values from 0.1 to 1.9
- spatial_second: bfloat16 [9, 128, 128], replicated, may hold values from -0.1875 to 0.1875
- temporal_second: bfloat16 [3, 128, 128], replicated, may hold values from -0.3125 to 0.3125
Outputs:
- encoded: bfloat16 [32, 256, 128, 128], P('tm', 'space')
The draws below stay inside these ranges and needn't reach their ends.
All inputs are finite; a program needn't handle non-finite values.
Results may differ from the reference program's by a relative error of at most 0.007.
Values may be sent and summed in bfloat16 or wider, within the bound.
A program may use at most 64 MiB of HBM per device.

```python
import math
import jax
import jax.numpy as jnp
from jax import lax

C = 128
G = 32
COLS = 128
FRAMES = 32
HEIGHT = 256


def draw_video(key, part):
    noise_key, row_key, col_key = jax.random.split(key, 3)
    row_index = jnp.arange(HEIGHT, dtype=jnp.float32)
    row_scale = 3.0 ** (row_index / max(HEIGHT - 1, 1)) * jnp.exp(jax.random.uniform(row_key, (HEIGHT,), jnp.float32, 0.0, math.log(2.2)))
    col_scale = jnp.exp(jax.random.uniform(col_key, (COLS,), jnp.float32, math.log(0.4), math.log(2.5)))
    full_shape = (FRAMES, HEIGHT, COLS, C)
    noise_part = jnp.clip(jax.random.normal(noise_key, full_shape, jnp.float32), -4.0, 4.0)
    cell_scale = 0.15 * row_scale[:, None, None] * col_scale[None, :, None]
    return (noise_part * cell_scale).astype(jnp.bfloat16)


def scatter_about(key, extent, scale, most, held_as=jnp.bfloat16):
    return jnp.clip(scale * jax.random.normal(key, extent, jnp.float32), -most, most).astype(held_as)


def setup_inputs(seed: int = 0) -> dict:
    arg_keys = jax.random.split(jax.random.key(seed), 8)
    return {
        "video": draw_video(jax.random.fold_in(arg_keys[7], 71), 0),
        "gain_first": jnp.clip(1.0 + 0.18 * jax.random.normal(arg_keys[1], (C,), jnp.float32), 0.1, 1.9),
        "spatial_first": scatter_about(arg_keys[2], (9, C, C), (9 * C) ** -0.5, 0.1875),
        "temporal_first": scatter_about(arg_keys[3], (3, C, C), (3 * C) ** -0.5, 0.3125),
        "gain_second": jnp.clip(1.0 + 0.18 * jax.random.normal(arg_keys[4], (C,), jnp.float32), 0.1, 1.9),
        "spatial_second": scatter_about(arg_keys[5], (9, C, C), (9 * C) ** -0.5, 0.1875),
        "temporal_second": scatter_about(arg_keys[6], (3, C, C), (3 * C) ** -0.5, 0.3125),
    }


norm_eps = 1e-06

def normalize_silu(values, gain):
    per_group = C // G

    def one_frame(frame):
        as_float = frame.astype(jnp.float32)
        totals = lax.optimization_barrier(jnp.sum(as_float, axis=(0, 1))).reshape(G, per_group).sum(axis=1)
        squares = lax.optimization_barrier(jnp.sum(as_float * as_float, axis=(0, 1))).reshape(G, per_group).sum(axis=1)
        members = frame.shape[0] * frame.shape[1] * per_group
        center = totals / members
        inverse = lax.rsqrt(squares / members - center * center + norm_eps)
        normed = (as_float - jnp.repeat(center, per_group)) * jnp.repeat(inverse, per_group) * gain
        return jax.nn.silu(normed).astype(jnp.bfloat16)
    return lax.map(one_frame, values)

def spatial_conv(values, weight):

    def one_frame(frame):
        tile_rows, tile_cols, channels = frame.shape
        padded = jnp.pad(frame, ((1, 1), (1, 1), (0, 0)))
        total = jnp.zeros((tile_rows, tile_cols, channels), jnp.float32)
        for row_shift in range(3):
            for col_shift in range(3):
                window = padded[row_shift:row_shift + tile_rows, col_shift:col_shift + tile_cols, :]
                total = total + jnp.dot(window, weight[3 * row_shift + col_shift], preferred_element_type=jnp.float32)
        return total.astype(jnp.bfloat16)
    return lax.map(one_frame, values)

def temporal_conv(values, weight, residual):
    padded = jnp.concatenate([values[:1], values[:1], values], axis=0)
    frames = values.shape[0]

    def one_frame(index):
        total = jnp.zeros(values.shape[1:], jnp.float32)
        for offset in range(3):
            frame = lax.dynamic_index_in_dim(padded, index + offset, 0, keepdims=False)
            total = total + jnp.dot(frame, weight[offset], preferred_element_type=jnp.float32)
        if residual is None:
            return total.astype(jnp.bfloat16)
        source = lax.dynamic_index_in_dim(residual, index, 0, keepdims=False)
        return (source.astype(jnp.float32) + total).astype(jnp.bfloat16)
    return lax.map(one_frame, jnp.arange(frames, dtype=jnp.int32))

def reference(video, gain_first, spatial_first, temporal_first, gain_second, spatial_second, temporal_second):
    active_first = normalize_silu(video, gain_first)
    spatial_out_first = spatial_conv(active_first, spatial_first)
    hidden = temporal_conv(spatial_out_first, temporal_first, None)
    active_second = normalize_silu(hidden, gain_second)
    spatial_out_second = spatial_conv(active_second, spatial_second)
    return temporal_conv(spatial_out_second, temporal_second, video)
```

```python
import jax
import jax.numpy as jnp
from jax import lax
from jax.experimental import pallas as pl
from jax.experimental.pallas import tpu as pltpu
from jax.sharding import PartitionSpec as P

G = 32
C = 128
norm_eps = 1e-06

F32 = jnp.float32
BF16 = jnp.bfloat16

PARTS = 2


def kernel(
    members,
    video, gain1, sp1, tp1, gain2, sp2, tp2, out,
    xin, act, s1, s2, hid, w1, w2, t1, t2, g1, g2, outb, st_send, st_recv,
    ld_sem, w_sem, st_ssem, st_rsem, h_ssem, h_rsem, s_ssem, s_rsem, out_sem,
):
    frames, rows, cols, _ = video.shape
    pairs = rows // 2
    n_space, n_tm = lax.axis_size("space"), lax.axis_size("tm")
    space, tm = lax.axis_index("space"), lax.axis_index("tm")
    has_up, has_down = space > 0, space < n_space - 1
    has_before, has_after = tm > 0, tm < n_tm - 1
    others = n_space - 1

    barrier = pltpu.get_barrier_semaphore()

    def greet(d, _):
        pl.semaphore_signal(barrier, 1, device_id={"space": lax.rem(space + d, n_space)})
        return 0

    lax.fori_loop(1, n_space, greet, 0)

    @pl.when(has_before)
    def _():
        pl.semaphore_signal(barrier, 1, device_id={"tm": tm - 1})

    @pl.when(has_after)
    def _():
        pl.semaphore_signal(barrier, 1, device_id={"tm": tm + 1})

    loads = [
        pltpu.make_async_copy(video.at[f], xin.at[f, pl.ds(1, rows)], ld_sem.at[f])
        for f in range(frames)
    ]
    for load in loads:
        load.start()
    weight_loads = [
        pltpu.make_async_copy(gain1, g1, w_sem.at[0]),
        pltpu.make_async_copy(sp1, w1.at[pl.ds(0, 9), :, pl.ds(0, C)], w_sem.at[1]),
        pltpu.make_async_copy(sp1, w1.at[pl.ds(3, 9), :, pl.ds(C, C)], w_sem.at[2]),
        pltpu.make_async_copy(tp1, t1.at[pl.ds(0, 3), :, pl.ds(0, C)], w_sem.at[3]),
        pltpu.make_async_copy(tp1, t1.at[pl.ds(1, 3), :, pl.ds(C, C)], w_sem.at[4]),
        pltpu.make_async_copy(gain2, g2, w_sem.at[5]),
        pltpu.make_async_copy(sp2, w2.at[pl.ds(0, 9), :, pl.ds(0, C)], w_sem.at[6]),
        pltpu.make_async_copy(sp2, w2.at[pl.ds(3, 9), :, pl.ds(C, C)], w_sem.at[7]),
        pltpu.make_async_copy(tp2, t2.at[pl.ds(0, 3), :, pl.ds(0, C)], w_sem.at[8]),
        pltpu.make_async_copy(tp2, t2.at[pl.ds(1, 3), :, pl.ds(C, C)], w_sem.at[9]),
    ]
    for load in weight_loads:
        load.start()
    for w in (w1, w2):
        w[pl.ds(9, 3), :, pl.ds(0, C)] = jnp.zeros((3, C, C), BF16)
        w[pl.ds(0, 3), :, pl.ds(C, C)] = jnp.zeros((3, C, C), BF16)
    for t in (t1, t2):
        t[pl.ds(3, 1), :, pl.ds(0, C)] = jnp.zeros((1, C, C), BF16)
        t[pl.ds(0, 1), :, pl.ds(C, C)] = jnp.zeros((1, C, C), BF16)

    def moments(x):
        x = x.reshape(-1, 8, C)
        return (
            jnp.sum(jnp.sum(x, axis=0), axis=0, keepdims=True),
            jnp.sum(jnp.sum(x * x, axis=0), axis=0, keepdims=True),
        )

    def exchange(k):
        def send(d, _):
            pltpu.make_async_remote_copy(
                st_send.at[k],
                st_recv.at[k, d - 1],
                st_ssem.at[k],
                st_rsem.at[k],
                device_id={"space": lax.rem(space + d, n_space)},
            ).start()
            return 0

        lax.fori_loop(1, n_space, send, 0)

    def all_sums(k):
        whole = st_recv.at[k, pl.ds(0, others)]
        pltpu.make_async_copy(whole, whole, st_rsem.at[k]).wait()
        total = st_send[k] + jnp.sum(st_recv[k], axis=0)
        lane = lax.broadcasted_iota(jnp.int32, (8, C), 1)
        size = C // G
        step = 1
        while step < size:
            low = lax.rem(lane, 2 * step) < step
            total = total + jnp.where(
                low, pltpu.roll(total, C - step, 1), pltpu.roll(total, step, 1)
            )
            step *= 2
        return total

    def scales(total, n, gain):
        center = total[0:n] / members
        inverse = lax.rsqrt(total[n : 2 * n] / members - center * center + norm_eps)
        return center, inverse * gain * 0.5

    first_col = lax.broadcasted_iota(jnp.int32, (cols, C), 0) == 0
    last_col = lax.broadcasted_iota(jnp.int32, (cols, C), 0) == cols - 1

    def activate(src, f, q, center, half):
        h = (src[f, q].astype(F32) - center) * half
        a = h * (1.0 + jnp.tanh(h))
        left = jnp.where(first_col, 0.0, pltpu.roll(a, 1, 0))
        right = jnp.where(last_col, 0.0, pltpu.roll(a, cols - 1, 0))
        act[f, q // 2, q % 2, :, pl.ds(0, C)] = left.astype(BF16)
        act[f, q // 2, q % 2, :, pl.ds(C, C)] = a.astype(BF16)
        act[f, q // 2, q % 2, :, pl.ds(2 * C, C)] = right.astype(BF16)

    def activate_tile(src, f, center, half):
        def step(p, _):
            for o in (1, 2):
                activate(src, f, 2 * p + o, center, half)
            return 0

        lax.fori_loop(0, pairs, step, 0)

    def halo_copies(k, src, src_up, src_down, dst, lo, n):
        up = pltpu.make_async_remote_copy(
            src.at[pl.ds(lo, n), src_up],
            dst.at[pl.ds(lo, n), rows + 1],
            h_ssem.at[k, 0],
            h_rsem.at[k, 0],
            device_id={"space": lax.max(space - 1, 0)},
        )
        down = pltpu.make_async_remote_copy(
            src.at[pl.ds(lo, n), src_down],
            dst.at[pl.ds(lo, n), 0],
            h_ssem.at[k, 1],
            h_rsem.at[k, 1],
            device_id={"space": lax.min(space + 1, n_space - 1)},
        )
        return up, down

    def send_halo(copies):
        up, down = copies

        @pl.when(has_up)
        def _():
            up.start()

        @pl.when(has_down)
        def _():
            down.start()

    def wait_halo_in(copies):
        up, down = copies

        @pl.when(has_down)
        def _():
            up.wait_recv()

        @pl.when(has_up)
        def _():
            down.wait_recv()

    def wait_halo_out(copies):
        up, down = copies

        @pl.when(has_up)
        def _():
            up.wait_send()

        @pl.when(has_down)
        def _():
            down.wait_send()

    def activate_halo(src, fs):
        for present, q in ((has_up, 0), (has_down, rows + 1)):

            @pl.when(present)
            def _():
                for f, center, half in fs:
                    activate(src, f, q, center, half)

            @pl.when(jnp.logical_not(present))
            def _():
                for f, _c, _h in fs:
                    act[f, q // 2, q % 2] = jnp.zeros((cols, 3 * C), BF16)

    np_ = pairs // PARTS

    def spatial(w, s, f0, part):
        p0 = part * np_
        lhs = jnp.concatenate(
            [
                act[pl.ds(f0, 2), pl.ds(p0 + i // 2, np_), i % 2].reshape(2 * np_ * cols, 3 * C)
                for i in range(4)
            ],
            axis=1,
        )
        o = jnp.dot(lhs, w[...].reshape(12 * C, 2 * C), preferred_element_type=F32)
        o = o.astype(BF16).reshape(2, np_, cols, 2 * C)
        s[pl.ds(2 + f0, 2), pl.ds(p0, np_), 0] = o[..., :C]
        s[pl.ds(2 + f0, 2), pl.ds(p0, np_), 1] = o[..., C:]

    def temporal(t, s, f0, part):
        p0 = part * np_
        lhs = jnp.concatenate(
            [s[f0 + i, pl.ds(p0, np_)].reshape(2 * np_ * cols, C) for i in range(4)], axis=1
        )
        return jnp.dot(lhs, t[...].reshape(4 * C, 2 * C), preferred_element_type=F32)

    def carry_copy(k, s, part):
        here = pl.ds(part * np_, np_)
        return pltpu.make_async_remote_copy(
            s.at[pl.ds(frames, 2), here],
            s.at[pl.ds(0, 2), here],
            s_ssem.at[k, part],
            s_rsem.at[k, part],
            device_id={"tm": lax.min(tm + 1, n_tm - 1)},
        )

    def carry(k, s, part):
        copy = carry_copy(k, s, part)

        @pl.when(has_after)
        def _():
            copy.start()

    def carried(k, s, part):
        copy = carry_copy(k, s, part)

        @pl.when(has_before)
        def _():
            copy.wait_recv()

        @pl.when(jnp.logical_not(has_before))
        def _():
            here = pl.ds(part * np_, np_)
            s[0, here] = s[2, here]
            s[1, here] = s[2, here]

    def hidden_part(f0, part):
        h = temporal(t1, s1, f0, part).astype(BF16)
        own = pl.ds(1 + part * 2 * np_, 2 * np_)
        sums = []
        for j in range(2):
            hj = h[:, j * C : (j + 1) * C]
            hid[f0 + j, own] = hj.reshape(2 * np_, cols, C)
            sums.append(moments(hj.astype(F32)))
        return [sums[0][0], sums[1][0], sums[0][1], sums[1][1]]

    def hidden(k, f0):
        sums = None
        for part in range(PARTS):
            if f0 == 0:
                carried(0, s1, part)
            new = hidden_part(f0, part)
            sums = new if sums is None else [a + b for a, b in zip(sums, new)]
        st_send[k] = jnp.concatenate(sums + [jnp.zeros((4, C), F32)], axis=0)
        exchange(k)
        copies = halo_copies(k, hid, 1, rows, hid, f0, 2)
        send_halo(copies)
        return copies

    def second(k, f0, copies):
        center, half = scales(all_sums(k), 2, g2[...].reshape(1, C))
        fs = [(f0 + j, center[j : j + 1], half[j : j + 1]) for j in range(2)]
        for f in fs:
            activate_tile(hid, *f)
        wait_halo_in(copies)
        activate_halo(hid, fs)

    out_copies = []

    def finish(f0, part):
        r = temporal(t2, s2, f0, part)
        rows_here = 2 * np_
        r0 = part * rows_here
        for j in range(2):
            v = xin[f0 + j, pl.ds(1 + r0, rows_here)].astype(F32)
            total = v + r[:, j * C : (j + 1) * C].reshape(rows_here, cols, C)
            outb[f0 + j, pl.ds(r0, rows_here)] = total.astype(BF16)
        here = (pl.ds(f0, 2), pl.ds(r0, rows_here))
        copy = pltpu.make_async_copy(outb.at[here], out.at[here], out_sem.at[f0 // 2, part])
        copy.start()
        out_copies.append(copy)

    sums = []
    for f in range(frames):
        loads[f].wait()

        def add(p, c, f=f):
            x = xin[f, pl.ds(1 + 2 * p, 2)].astype(F32).reshape(-1, 8, C)
            return c[0] + jnp.sum(x, axis=0), c[1] + jnp.sum(x * x, axis=0)

        zero = jnp.zeros((8, C), F32)
        a, b = lax.fori_loop(0, pairs, add, (zero, zero))
        sums.append((jnp.sum(a, axis=0, keepdims=True), jnp.sum(b, axis=0, keepdims=True)))
    st_send[0] = jnp.concatenate([s[0] for s in sums] + [s[1] for s in sums], axis=0)

    greeted = others + has_before.astype(jnp.int32) + has_after.astype(jnp.int32)
    pl.semaphore_wait(barrier, greeted)
    exchange(0)
    halo0 = halo_copies(0, video, 0, rows - 1, xin, 0, frames)
    send_halo(halo0)

    for load in weight_loads:
        load.wait()
    center, half = scales(all_sums(0), 4, g1[...].reshape(1, C))
    fs = [(f, center[f : f + 1], half[f : f + 1]) for f in range(frames)]
    for f in (2, 3):
        activate_tile(xin, *fs[f])
    wait_halo_in(halo0)
    activate_halo(xin, fs)
    for part in range(PARTS):
        spatial(w1, s1, 2, part)
        carry(0, s1, part)
    for f in (0, 1):
        activate_tile(xin, *fs[f])
    for part in range(PARTS):
        spatial(w1, s1, 0, part)

    halo1 = hidden(1, 2)
    second(1, 2, halo1)
    for part in range(PARTS):
        spatial(w2, s2, 2, part)
        carry(1, s2, part)

    halo2 = hidden(2, 0)
    second(2, 0, halo2)
    for part in range(PARTS):
        spatial(w2, s2, 0, part)
    for part in range(PARTS):
        finish(2, part)
    for part in range(PARTS):
        carried(1, s2, part)
        finish(0, part)

    for k, copies in enumerate((halo0, halo1, halo2)):
        wait_halo_out(copies)
        whole = st_recv.at[k, pl.ds(0, others)]
        pltpu.make_async_copy(whole, whole, st_ssem.at[k]).wait()
    for k, s in ((0, s1), (1, s2)):
        for part in range(PARTS):
            copy = carry_copy(k, s, part)

            @pl.when(has_after)
            def _():
                copy.wait_send()
    for copy in out_copies:
        copy.wait()


def shards(video, gain1, sp1, tp1, gain2, sp2, tp2):
    frames, rows, cols, channels = video.shape
    n_space = lax.axis_size("space")
    members = rows * n_space * cols * (channels // G)
    any_spec = pl.BlockSpec(memory_space=pl.ANY)
    call = pl.pallas_call(
        lambda *refs: kernel(float(members), *refs),
        out_shape=jax.ShapeDtypeStruct(video.shape, BF16),
        in_specs=[any_spec] * 7,
        out_specs=any_spec,
        scratch_shapes=[
            pltpu.VMEM((frames, rows + 2, cols, C), BF16),
            pltpu.VMEM((frames, rows // 2 + 1, 2, cols, 3 * C), BF16),
            pltpu.VMEM((frames + 2, rows // 2, 2, cols, C), BF16),
            pltpu.VMEM((frames + 2, rows // 2, 2, cols, C), BF16),
            pltpu.VMEM((frames, rows + 2, cols, C), BF16),
            pltpu.VMEM((12, C, 2 * C), BF16),
            pltpu.VMEM((12, C, 2 * C), BF16),
            pltpu.VMEM((4, C, 2 * C), BF16),
            pltpu.VMEM((4, C, 2 * C), BF16),
            pltpu.VMEM((C,), F32),
            pltpu.VMEM((C,), F32),
            pltpu.VMEM((frames, rows, cols, C), BF16),
            pltpu.VMEM((3, 8, C), F32),
            pltpu.VMEM((3, n_space - 1, 8, C), F32),
            pltpu.SemaphoreType.DMA((frames,)),
            pltpu.SemaphoreType.DMA((10,)),
            pltpu.SemaphoreType.DMA((3,)),
            pltpu.SemaphoreType.DMA((3,)),
            pltpu.SemaphoreType.DMA((3, 2)),
            pltpu.SemaphoreType.DMA((3, 2)),
            pltpu.SemaphoreType.DMA((2, PARTS)),
            pltpu.SemaphoreType.DMA((2, PARTS)),
            pltpu.SemaphoreType.DMA((2, PARTS)),
        ],
        compiler_params=pltpu.CompilerParams(
            collective_id=0, has_side_effects=True, vmem_limit_bytes=48 * 2**20
        ),
        cost_estimate=pl.CostEstimate(
            flops=4 * 10**9, bytes_accessed=4 * 2**20, transcendentals=10**6
        ),
        name="block",
    )
    return call(video, gain1, sp1, tp1, gain2, sp2, tp2)


def solution(mesh):
    in_specs = (P("tm", "space", None, None), P(), P(), P(), P(), P(), P())
    out_specs = P("tm", "space", None, None)
    return jax.shard_map(shards, mesh=mesh, in_specs=in_specs, out_specs=out_specs, check_vma=False)
```

```python
import jax
import jax.numpy as jnp
from jax import lax
from jax.experimental import pallas as pl
from jax.experimental.pallas import tpu as pltpu
from jax.sharding import PartitionSpec as P

G = 32
C = 128
norm_eps = 1e-06

F32 = jnp.float32
BF16 = jnp.bfloat16

PARTS = 2


def kernel(
    members,
    video, gain1, sp1, tp1, gain2, sp2, tp2, out,
    xin, act, s1, s2, hid, w1, w2, t1, t2, g1, g2, st_send, st_recv, tot_send, tot_recv, relay,
    ld_sem, w_sem, st_ssem, st_rsem, h_ssem, h_rsem, y_ssem, y_rsem, rl_ssem, rl_rsem,
):
    frames, rows, cols, _ = video.shape
    pairs = rows // 2
    n_space, n_tm = lax.axis_size("space"), lax.axis_size("tm")
    space, tm = lax.axis_index("space"), lax.axis_index("tm")
    has_up, has_down = space > 0, space < n_space - 1
    has_before, has_after = tm > 0, tm < n_tm - 1
    cross = n_tm // 2 - 1
    crossing = tm == cross
    straight = jnp.logical_and(has_after, jnp.logical_not(crossing))
    relaying = tm == 0
    relayed = tm == cross + 1
    others = n_space - 1

    barrier = pltpu.get_barrier_semaphore()

    def greet(d, _):
        pl.semaphore_signal(barrier, 1, device_id={"space": lax.rem(space + d, n_space)})
        return 0

    lax.fori_loop(1, n_space, greet, 0)

    @pl.when(has_before)
    def _():
        pl.semaphore_signal(barrier, 1, device_id={"tm": tm - 1})

    @pl.when(has_after)
    def _():
        pl.semaphore_signal(barrier, 1, device_id={"tm": tm + 1})

    @pl.when(relaying)
    def _():
        pl.semaphore_signal(barrier, 1, device_id={"tm": cross})
        pl.semaphore_signal(barrier, 1, device_id={"tm": cross + 1})

    @pl.when(jnp.logical_or(crossing, relayed))
    def _():
        pl.semaphore_signal(barrier, 1, device_id={"tm": 0})

    loads = [
        pltpu.make_async_copy(video.at[f], xin.at[2 + f, pl.ds(1, rows)], ld_sem.at[f])
        for f in range(frames)
    ]
    for load in loads:
        load.start()
    weight_loads = [
        pltpu.make_async_copy(gain1, g1, w_sem.at[0]),
        pltpu.make_async_copy(sp1, w1.at[pl.ds(0, 9), :, pl.ds(0, C)], w_sem.at[1]),
        pltpu.make_async_copy(sp1, w1.at[pl.ds(3, 9), :, pl.ds(C, C)], w_sem.at[2]),
        pltpu.make_async_copy(tp1, t1.at[pl.ds(0, 3), :, pl.ds(0, C)], w_sem.at[3]),
        pltpu.make_async_copy(tp1, t1.at[pl.ds(1, 3), :, pl.ds(C, C)], w_sem.at[4]),
        pltpu.make_async_copy(gain2, g2, w_sem.at[5]),
        pltpu.make_async_copy(sp2, w2.at[pl.ds(0, 9), :, pl.ds(0, C)], w_sem.at[6]),
        pltpu.make_async_copy(sp2, w2.at[pl.ds(3, 9), :, pl.ds(C, C)], w_sem.at[7]),
        pltpu.make_async_copy(tp2, t2.at[pl.ds(0, 3), :, pl.ds(0, C)], w_sem.at[8]),
        pltpu.make_async_copy(tp2, t2.at[pl.ds(1, 3), :, pl.ds(C, C)], w_sem.at[9]),
    ]
    for load in weight_loads:
        load.start()
    for w in (w1, w2):
        w[pl.ds(9, 3), :, pl.ds(0, C)] = jnp.zeros((3, C, C), BF16)
        w[pl.ds(0, 3), :, pl.ds(C, C)] = jnp.zeros((3, C, C), BF16)
    for t in (t1, t2):
        t[pl.ds(3, 1), :, pl.ds(0, C)] = jnp.zeros((1, C, C), BF16)
        t[pl.ds(0, 1), :, pl.ds(C, C)] = jnp.zeros((1, C, C), BF16)

    def moments(x):
        x = x.reshape(-1, 8, C)
        return (
            jnp.sum(jnp.sum(x, axis=0), axis=0, keepdims=True),
            jnp.sum(jnp.sum(x * x, axis=0), axis=0, keepdims=True),
        )

    group = C // G
    lane = lax.broadcasted_iota(jnp.int32, (1, C), 1)

    def over_group(x):
        step = 1
        while step < group:
            low = lax.rem(lane, 2 * step) < step
            x = x + jnp.where(low, pltpu.roll(x, C - step, 1), pltpu.roll(x, step, 1))
            step *= 2
        return x

    def pack(rows_in):
        packed = jnp.zeros((1, C), F32)
        for i, x in enumerate(rows_in):
            packed = jnp.where(lax.rem(lane, group) == i, over_group(x), packed)
        return packed

    def unpack(packed, i):
        return over_group(jnp.where(lax.rem(lane, group) == i, packed, 0.0))

    def sizes(k):
        return 2 if k == 0 else 1

    def exchange(k, packed):
        n = sizes(k)
        for i, x in enumerate(packed):
            st_send[k, pl.ds(i, 1)] = x

        def send(d, _):
            pltpu.make_async_remote_copy(
                st_send.at[k, pl.ds(0, n)],
                st_recv.at[k, d - 1, pl.ds(0, n)],
                st_ssem.at[k],
                st_rsem.at[k],
                device_id={"space": lax.rem(space + d, n_space)},
            ).start()
            return 0

        lax.fori_loop(1, n_space, send, 0)

    def all_sums(k):
        n = sizes(k)
        whole = st_recv.at[k, pl.ds(0, others), pl.ds(0, n)]
        pltpu.make_async_copy(whole, whole, st_rsem.at[k]).wait()
        return [
            st_send[k, pl.ds(i, 1)] + jnp.sum(st_recv[k, :, pl.ds(i, 1)], axis=0) for i in range(n)
        ]

    def scales(total, square, gain):
        center = total / members
        inverse = lax.rsqrt(square / members - center * center + norm_eps)
        return center, inverse * gain * 0.5

    first_col = lax.broadcasted_iota(jnp.int32, (cols, C), 0) == 0
    last_col = lax.broadcasted_iota(jnp.int32, (cols, C), 0) == cols - 1

    def activate(src, f, q, center, half):
        h = (src[f, q].astype(F32) - center) * half
        a = h * (1.0 + jnp.tanh(h))
        left = jnp.where(first_col, 0.0, pltpu.roll(a, 1, 0))
        right = jnp.where(last_col, 0.0, pltpu.roll(a, cols - 1, 0))
        act[f, q // 2, q % 2, :, pl.ds(0, C)] = left.astype(BF16)
        act[f, q // 2, q % 2, :, pl.ds(C, C)] = a.astype(BF16)
        act[f, q // 2, q % 2, :, pl.ds(2 * C, C)] = right.astype(BF16)

    def activate_tile(src, f, center, half):
        def step(p, _):
            for o in (1, 2):
                activate(src, f, 2 * p + o, center, half)
            return 0

        lax.fori_loop(0, pairs, step, 0)

    def halo_copies(k, buf, e, n):
        up = pltpu.make_async_remote_copy(
            buf.at[pl.ds(e, n), 1],
            buf.at[pl.ds(e, n), rows + 1],
            h_ssem.at[k, 0],
            h_rsem.at[k, 0],
            device_id={"space": lax.max(space - 1, 0)},
        )
        down = pltpu.make_async_remote_copy(
            buf.at[pl.ds(e, n), rows],
            buf.at[pl.ds(e, n), 0],
            h_ssem.at[k, 1],
            h_rsem.at[k, 1],
            device_id={"space": lax.min(space + 1, n_space - 1)},
        )
        return up, down

    def send_halo(copies):
        up, down = copies

        @pl.when(has_up)
        def _():
            up.start()

        @pl.when(has_down)
        def _():
            down.start()

    def wait_halo_in(copies):
        up, down = copies

        @pl.when(has_down)
        def _():
            up.wait_recv()

        @pl.when(has_up)
        def _():
            down.wait_recv()

    def wait_halo_out(copies):
        up, down = copies

        @pl.when(has_up)
        def _():
            up.wait_send()

        @pl.when(has_down)
        def _():
            down.wait_send()

    def activate_halo(src, fs):
        for present, q in ((has_up, 0), (has_down, rows + 1)):

            @pl.when(present)
            def _():
                for f, center, half in fs:
                    activate(src, f, q, center, half)

            @pl.when(jnp.logical_not(present))
            def _():
                for f, _c, _h in fs:
                    act[f, q // 2, q % 2] = jnp.zeros((cols, 3 * C), BF16)

    np_ = pairs // PARTS

    def spatial(w, s, e, part):
        p0 = part * np_
        lhs = jnp.concatenate(
            [
                act[pl.ds(e, 2), pl.ds(p0 + i // 2, np_), i % 2].reshape(2 * np_ * cols, 3 * C)
                for i in range(4)
            ],
            axis=1,
        )
        o = jnp.dot(lhs, w[...].reshape(12 * C, 2 * C), preferred_element_type=F32)
        o = o.astype(BF16).reshape(2, np_, cols, 2 * C)
        s[pl.ds(e, 2), pl.ds(p0, np_), 0] = o[..., :C]
        s[pl.ds(e, 2), pl.ds(p0, np_), 1] = o[..., C:]

    def temporal(t, s, e, part):
        p0 = part * np_
        lhs = jnp.concatenate(
            [s[e - 2 + i, pl.ds(p0, np_)].reshape(2 * np_ * cols, C) for i in range(4)], axis=1
        )
        return jnp.dot(lhs, t[...].reshape(4 * C, 2 * C), preferred_element_type=F32)

    mid = rows // 2
    pieces = [(1, 1), (rows, 1), (2, mid - 1), (mid + 1, mid - 1)]
    last = len(pieces) - 1
    total_at = len(pieces)

    def onward(k, buf, piece):
        r, n = pieces[piece]
        return pltpu.make_async_remote_copy(
            buf.at[pl.ds(frames, 2), pl.ds(r, n)],
            buf.at[pl.ds(0, 2), pl.ds(r, n)],
            y_ssem.at[k, piece],
            y_rsem.at[k, piece],
            device_id={"tm": lax.min(tm + 1, n_tm - 1)},
        )

    def onward_total(k):
        return pltpu.make_async_remote_copy(
            tot_send.at[k],
            tot_recv.at[k],
            y_ssem.at[k, total_at],
            y_rsem.at[k, total_at],
            device_id={"tm": lax.min(tm + 1, n_tm - 1)},
        )

    def to_relay(k, buf):
        r, n = pieces[last]
        return pltpu.make_async_remote_copy(
            buf.at[pl.ds(frames, 2), pl.ds(r, n)],
            relay.at[k],
            y_ssem.at[k, last],
            rl_rsem.at[k],
            device_id={"tm": 0},
        )

    def from_relay(k, buf):
        r, n = pieces[last]
        return pltpu.make_async_remote_copy(
            relay.at[k],
            buf.at[pl.ds(0, 2), pl.ds(r, n)],
            rl_ssem.at[k],
            y_rsem.at[k, last],
            device_id={"tm": cross + 1},
        )

    def send_total(k, packed):
        tot_send[k] = packed

        @pl.when(has_after)
        def _():
            onward_total(k).start()

    def pass_edges(k, buf, copies):
        @pl.when(has_before)
        def _():
            onward(k, buf, 0).wait_recv()
            onward(k, buf, 1).wait_recv()
            send_halo(copies)

    def pass_relay(k, buf):
        @pl.when(relaying)
        def _():
            to_relay(k, buf).wait_recv()
            from_relay(k, buf).start()

    def earlier_scales(k, gain):
        onward_total(k).wait_recv()
        packed = tot_recv[k]
        return pair_scales(packed, gain)

    def pair_scales(packed, gain):
        return [scales(unpack(packed, j), unpack(packed, 2 + j), gain) for j in range(2)]

    def activate_pair(src, e, pair, copies):
        fs = [(e + j, *pair[j]) for j in range(2)]
        for f in fs:
            activate_tile(src, *f)
        if copies is not None:
            wait_halo_in(copies)
        activate_halo(src, fs)

    def earlier(k, buf, w, s, gain, copies):
        @pl.when(has_before)
        def _():
            pair = earlier_scales(k, gain)
            for piece in (2, 3):
                onward(k, buf, piece).wait_recv()
            activate_pair(buf, 0, pair, copies)
            for part in range(PARTS):
                spatial(w, s, 0, part)

        @pl.when(jnp.logical_not(has_before))
        def _():
            s[0] = s[2]
            s[1] = s[2]

    def hidden_part(e, part):
        h = temporal(t1, s1, e, part).astype(BF16)
        own = pl.ds(1 + part * 2 * np_, 2 * np_)
        sums = []
        for j in range(2):
            hj = h[:, j * C : (j + 1) * C]
            hid[e + j, own] = hj.reshape(2 * np_, cols, C)
            sums.append(moments(hj.astype(F32)))
        return [sums[0][0], sums[1][0], sums[0][1], sums[1][1]]

    def hidden(k, e):
        sums = None
        for part in range(PARTS):
            new = hidden_part(e, part)
            sums = new if sums is None else [a + b for a, b in zip(sums, new)]
        exchange(k, [pack(sums)])

    def finish(f0, part):
        r = temporal(t2, s2, 2 + f0, part)
        rows_here = 2 * np_
        r0 = part * rows_here
        for j in range(2):
            v = xin[2 + f0 + j, pl.ds(1 + r0, rows_here)].astype(F32)
            total = v + r[:, j * C : (j + 1) * C].reshape(rows_here, cols, C)
            out[f0 + j, pl.ds(r0, rows_here)] = total.astype(BF16)

    sums = []
    for f in range(frames):
        loads[f].wait()

        def add(p, c, f=f):
            x = xin[2 + f, pl.ds(1 + 2 * p, 2)].astype(F32).reshape(-1, 8, C)
            return c[0] + jnp.sum(x, axis=0), c[1] + jnp.sum(x * x, axis=0)

        zero = jnp.zeros((8, C), F32)
        a, b = lax.fori_loop(0, pairs, add, (zero, zero))
        sums.append((jnp.sum(a, axis=0, keepdims=True), jnp.sum(b, axis=0, keepdims=True)))
    packed = [
        pack([sums[f][0], sums[f + 1][0], sums[f][1], sums[f + 1][1]]) for f in range(0, frames, 2)
    ]

    greeted = others + has_before.astype(jnp.int32) + has_after.astype(jnp.int32)
    greeted = greeted + 2 * relaying.astype(jnp.int32)
    greeted = greeted + crossing.astype(jnp.int32) + relayed.astype(jnp.int32)
    pl.semaphore_wait(barrier, greeted)
    exchange(0, packed)
    halo0 = halo_copies(0, xin, 2, frames)
    halo1 = halo_copies(1, hid, 4, 2)
    halo2 = halo_copies(2, hid, 2, 2)
    halo3 = halo_copies(3, xin, 0, 2)
    halo4 = halo_copies(4, hid, 0, 2)

    @pl.when(straight)
    def _():
        for piece in range(len(pieces)):
            onward(0, xin, piece).start()

    @pl.when(crossing)
    def _():
        to_relay(0, xin).start()
        onward(0, xin, 0).start()
        onward(0, xin, 1).start()

    send_halo(halo0)

    @pl.when(crossing)
    def _():
        onward(0, xin, 2).start()

    for load in weight_loads:
        load.wait()
    gain_first = g1[...].reshape(1, C)
    gain_second = g2[...].reshape(1, C)
    pass_relay(0, xin)
    pass_edges(0, xin, halo3)
    whole01, whole23 = all_sums(0)
    send_total(0, whole23)
    pair01, pair23 = pair_scales(whole01, gain_first), pair_scales(whole23, gain_first)

    activate_pair(xin, 4, pair23, halo0)
    for part in range(PARTS):
        spatial(w1, s1, 4, part)
    activate_pair(xin, 2, pair01, None)
    for part in range(PARTS):
        spatial(w1, s1, 2, part)
    hidden(1, 4)

    @pl.when(straight)
    def _():
        for piece in range(len(pieces) - 1):
            onward(1, hid, piece).start()

    @pl.when(crossing)
    def _():
        to_relay(1, hid).start()
        onward(1, hid, 0).start()
        onward(1, hid, 1).start()

    send_halo(halo1)

    @pl.when(crossing)
    def _():
        onward(1, hid, 2).start()

    earlier(0, xin, w1, s1, gain_first, halo3)
    hidden(2, 2)
    send_halo(halo2)

    (whole23,) = all_sums(1)
    send_total(1, whole23)

    @pl.when(straight)
    def _():
        onward(1, hid, last).start()

    activate_pair(hid, 4, pair_scales(whole23, gain_second), halo1)
    for part in range(PARTS):
        spatial(w2, s2, 4, part)
    pass_relay(1, hid)
    pass_edges(1, hid, halo4)

    (whole01,) = all_sums(2)
    activate_pair(hid, 2, pair_scales(whole01, gain_second), halo2)
    for part in range(PARTS):
        spatial(w2, s2, 2, part)
    for part in range(PARTS):
        finish(2, part)
    earlier(1, hid, w2, s2, gain_second, halo4)
    for part in range(PARTS):
        finish(0, part)

    for copies in (halo0, halo1, halo2):
        wait_halo_out(copies)
    for k in range(3):
        whole = st_recv.at[k, pl.ds(0, others), pl.ds(0, sizes(k))]
        pltpu.make_async_copy(whole, whole, st_ssem.at[k]).wait()

    @pl.when(has_before)
    def _():
        for copies in (halo3, halo4):
            wait_halo_out(copies)

    @pl.when(has_after)
    def _():
        for k, buf in ((0, xin), (1, hid)):
            for piece in range(len(pieces)):
                onward(k, buf, piece).wait_send()
            onward_total(k).wait_send()

    @pl.when(relaying)
    def _():
        for k, buf in ((0, xin), (1, hid)):
            from_relay(k, buf).wait_send()


def shards(video, gain1, sp1, tp1, gain2, sp2, tp2):
    frames, rows, cols, channels = video.shape
    n_space = lax.axis_size("space")
    members = rows * n_space * cols * (channels // G)
    hbm = pl.BlockSpec(memory_space=pltpu.HBM)
    inputs = (video, gain1, sp1, tp1, gain2, sp2, tp2)
    call = pl.pallas_call(
        lambda *refs: kernel(float(members), *refs),
        out_shape=pltpu.VMEM(video.shape, BF16),
        in_specs=[hbm] * 7,
        out_specs=pl.BlockSpec(memory_space=pltpu.VMEM),
        scratch_shapes=[
            pltpu.VMEM((frames + 2, rows + 2, cols, C), BF16),
            pltpu.VMEM((frames + 2, rows // 2 + 1, 2, cols, 3 * C), BF16),
            pltpu.VMEM((frames + 2, rows // 2, 2, cols, C), BF16),
            pltpu.VMEM((frames + 2, rows // 2, 2, cols, C), BF16),
            pltpu.VMEM((frames + 2, rows + 2, cols, C), BF16),
            pltpu.VMEM((12, C, 2 * C), BF16),
            pltpu.VMEM((12, C, 2 * C), BF16),
            pltpu.VMEM((4, C, 2 * C), BF16),
            pltpu.VMEM((4, C, 2 * C), BF16),
            pltpu.VMEM((C,), F32),
            pltpu.VMEM((C,), F32),
            pltpu.VMEM((3, 8, C), F32),
            pltpu.VMEM((3, n_space - 1, 8, C), F32),
            pltpu.VMEM((2, 1, C), F32),
            pltpu.VMEM((2, 1, C), F32),
            pltpu.VMEM((2, 2, rows // 2 - 1, cols, C), BF16),
            pltpu.SemaphoreType.DMA((frames,)),
            pltpu.SemaphoreType.DMA((10,)),
            pltpu.SemaphoreType.DMA((3,)),
            pltpu.SemaphoreType.DMA((3,)),
            pltpu.SemaphoreType.DMA((5, 2)),
            pltpu.SemaphoreType.DMA((5, 2)),
            pltpu.SemaphoreType.DMA((2, 5)),
            pltpu.SemaphoreType.DMA((2, 5)),
            pltpu.SemaphoreType.DMA((2,)),
            pltpu.SemaphoreType.DMA((2,)),
        ],
        compiler_params=pltpu.CompilerParams(
            collective_id=0, has_side_effects=True, vmem_limit_bytes=62 * 2**20
        ),
        cost_estimate=pl.CostEstimate(
            flops=4 * 10**9, bytes_accessed=4 * 2**20, transcendentals=10**6
        ),
        name="block",
    )
    return call(*[pltpu.with_memory_space_constraint(x, pltpu.HBM) for x in inputs])


def solution(mesh):
    in_specs = (P("tm", "space", None, None), P(), P(), P(), P(), P(), P())
    out_specs = P("tm", "space", None, None)
    return jax.shard_map(shards, mesh=mesh, in_specs=in_specs, out_specs=out_specs, check_vma=False)
```

```python
import jax
import jax.numpy as jnp
from jax import lax
from jax.experimental import pallas as pl
from jax.experimental.pallas import tpu as pltpu
from jax.sharding import PartitionSpec as P

G = 32
C = 128
norm_eps = 1e-06

F32 = jnp.float32
BF16 = jnp.bfloat16

PARTS = 2


def steps(n_space):
    n_x = n_space // 8

    def hops(step):
        x, z, core = step
        return min(x, n_x - x) + 2 * min(z, 4 - z) + core / 4

    every = [(x, z, core) for x in range(n_x) for z in range(4) for core in range(2)]
    return sorted((s for s in every if s != (0, 0, 0)), key=hops, reverse=True)


def kernel(
    members,
    video, gain1, sp1, tp1, gain2, sp2, tp2, out,
    xin, act, s1, s2, hid, w1, w2, t1, t2, g1, g2, st_send, st_recv, tot_send, tot_recv, relay,
    ld_sem, w_sem, st_ssem, st_rsem, h_ssem, h_rsem, y_ssem, y_rsem, rl_ssem, rl_rsem,
):
    frames, rows, cols, _ = video.shape
    pairs = rows // 2
    n_space, n_tm = lax.axis_size("space"), lax.axis_size("tm")
    space, tm = lax.axis_index("space"), lax.axis_index("tm")
    has_up, has_down = space > 0, space < n_space - 1
    has_before, has_after = tm > 0, tm < n_tm - 1
    cross = n_tm // 2 - 1
    crossing = tm == cross
    straight = jnp.logical_and(has_after, jnp.logical_not(crossing))
    relaying = tm == 0
    relayed = tm == cross + 1
    others = n_space - 1
    apart = steps(n_space)

    def tile(place):
        x, z, core = apart[place]
        across = lax.rem(space // 8 + x, n_space // 8)
        along = lax.rem(lax.rem(space // 2, 4) + z, 4)
        return across * 8 + along * 2 + lax.rem(space + core, 2)

    barrier = pltpu.get_barrier_semaphore()

    for place in range(others):
        pl.semaphore_signal(barrier, 1, device_id={"space": tile(place)})

    @pl.when(has_before)
    def _():
        pl.semaphore_signal(barrier, 1, device_id={"tm": tm - 1})

    @pl.when(has_after)
    def _():
        pl.semaphore_signal(barrier, 1, device_id={"tm": tm + 1})

    @pl.when(relaying)
    def _():
        pl.semaphore_signal(barrier, 1, device_id={"tm": cross})
        pl.semaphore_signal(barrier, 1, device_id={"tm": cross + 1})

    @pl.when(jnp.logical_or(crossing, relayed))
    def _():
        pl.semaphore_signal(barrier, 1, device_id={"tm": 0})

    loads = [
        pltpu.make_async_copy(video.at[f], xin.at[2 + f, pl.ds(1, rows)], ld_sem.at[f])
        for f in range(frames)
    ]
    for load in loads:
        load.start()
    weight_loads = [
        pltpu.make_async_copy(gain1, g1, w_sem.at[0]),
        pltpu.make_async_copy(sp1, w1.at[pl.ds(0, 9), :, pl.ds(0, C)], w_sem.at[1]),
        pltpu.make_async_copy(sp1, w1.at[pl.ds(3, 9), :, pl.ds(C, C)], w_sem.at[2]),
        pltpu.make_async_copy(tp1, t1.at[pl.ds(0, 3), :, pl.ds(0, C)], w_sem.at[3]),
        pltpu.make_async_copy(tp1, t1.at[pl.ds(1, 3), :, pl.ds(C, C)], w_sem.at[4]),
        pltpu.make_async_copy(gain2, g2, w_sem.at[5]),
        pltpu.make_async_copy(sp2, w2.at[pl.ds(0, 9), :, pl.ds(0, C)], w_sem.at[6]),
        pltpu.make_async_copy(sp2, w2.at[pl.ds(3, 9), :, pl.ds(C, C)], w_sem.at[7]),
        pltpu.make_async_copy(tp2, t2.at[pl.ds(0, 3), :, pl.ds(0, C)], w_sem.at[8]),
        pltpu.make_async_copy(tp2, t2.at[pl.ds(1, 3), :, pl.ds(C, C)], w_sem.at[9]),
    ]
    for load in weight_loads:
        load.start()
    for w in (w1, w2):
        w[pl.ds(9, 3), :, pl.ds(0, C)] = jnp.zeros((3, C, C), BF16)
        w[pl.ds(0, 3), :, pl.ds(C, C)] = jnp.zeros((3, C, C), BF16)
    for t in (t1, t2):
        t[pl.ds(3, 1), :, pl.ds(0, C)] = jnp.zeros((1, C, C), BF16)
        t[pl.ds(0, 1), :, pl.ds(C, C)] = jnp.zeros((1, C, C), BF16)

    def moments(x):
        x = x.reshape(-1, 8, C)
        return (
            jnp.sum(jnp.sum(x, axis=0), axis=0, keepdims=True),
            jnp.sum(jnp.sum(x * x, axis=0), axis=0, keepdims=True),
        )

    group = C // G
    lane = lax.broadcasted_iota(jnp.int32, (1, C), 1)

    def over_group(x):
        step = 1
        while step < group:
            low = lax.rem(lane, 2 * step) < step
            x = x + jnp.where(low, pltpu.roll(x, C - step, 1), pltpu.roll(x, step, 1))
            step *= 2
        return x

    def pack(rows_in):
        packed = jnp.zeros((1, C), F32)
        for i, x in enumerate(rows_in):
            packed = jnp.where(lax.rem(lane, group) == i, over_group(x), packed)
        return packed

    def unpack(packed, i):
        return over_group(jnp.where(lax.rem(lane, group) == i, packed, 0.0))

    def sizes(k):
        return 2 if k == 0 else 1

    def exchange(k, packed):
        n = sizes(k)
        for i, x in enumerate(packed):
            st_send[k, pl.ds(i, 1)] = x

        for place in range(others):
            pltpu.make_async_remote_copy(
                st_send.at[k, pl.ds(0, n)],
                st_recv.at[k, place, pl.ds(0, n)],
                st_ssem.at[k],
                st_rsem.at[k],
                device_id={"space": tile(place)},
            ).start()

    def all_sums(k):
        n = sizes(k)
        whole = st_recv.at[k, pl.ds(0, others), pl.ds(0, n)]
        pltpu.make_async_copy(whole, whole, st_rsem.at[k]).wait()
        return [
            st_send[k, pl.ds(i, 1)] + jnp.sum(st_recv[k, :, pl.ds(i, 1)], axis=0) for i in range(n)
        ]

    def scales(total, square, gain):
        center = total / members
        inverse = lax.rsqrt(square / members - center * center + norm_eps)
        return center, inverse * gain * 0.5

    first_col = lax.broadcasted_iota(jnp.int32, (cols, C), 0) == 0
    last_col = lax.broadcasted_iota(jnp.int32, (cols, C), 0) == cols - 1

    def activate(src, f, q, center, half):
        h = (src[f, q].astype(F32) - center) * half
        a = h * (1.0 + jnp.tanh(h))
        left = jnp.where(first_col, 0.0, pltpu.roll(a, 1, 0))
        right = jnp.where(last_col, 0.0, pltpu.roll(a, cols - 1, 0))
        act[f, q // 2, q % 2, :, pl.ds(0, C)] = left.astype(BF16)
        act[f, q // 2, q % 2, :, pl.ds(C, C)] = a.astype(BF16)
        act[f, q // 2, q % 2, :, pl.ds(2 * C, C)] = right.astype(BF16)

    def activate_tile(src, f, center, half):
        def step(p, _):
            for o in (1, 2):
                activate(src, f, 2 * p + o, center, half)
            return 0

        lax.fori_loop(0, pairs, step, 0)

    def halo_copies(k, buf, e, n):
        up = pltpu.make_async_remote_copy(
            buf.at[pl.ds(e, n), 1],
            buf.at[pl.ds(e, n), rows + 1],
            h_ssem.at[k, 0],
            h_rsem.at[k, 0],
            device_id={"space": lax.max(space - 1, 0)},
        )
        down = pltpu.make_async_remote_copy(
            buf.at[pl.ds(e, n), rows],
            buf.at[pl.ds(e, n), 0],
            h_ssem.at[k, 1],
            h_rsem.at[k, 1],
            device_id={"space": lax.min(space + 1, n_space - 1)},
        )
        return up, down

    def send_halo(copies):
        up, down = copies

        @pl.when(has_up)
        def _():
            up.start()

        @pl.when(has_down)
        def _():
            down.start()

    def wait_halo_in(copies):
        up, down = copies

        @pl.when(has_down)
        def _():
            up.wait_recv()

        @pl.when(has_up)
        def _():
            down.wait_recv()

    def wait_halo_out(copies):
        up, down = copies

        @pl.when(has_up)
        def _():
            up.wait_send()

        @pl.when(has_down)
        def _():
            down.wait_send()

    def activate_halo(src, fs):
        for present, q in ((has_up, 0), (has_down, rows + 1)):

            @pl.when(present)
            def _():
                for f, center, half in fs:
                    activate(src, f, q, center, half)

            @pl.when(jnp.logical_not(present))
            def _():
                for f, _c, _h in fs:
                    act[f, q // 2, q % 2] = jnp.zeros((cols, 3 * C), BF16)

    np_ = pairs // PARTS

    def spatial(w, s, e, part):
        p0 = part * np_
        lhs = jnp.concatenate(
            [
                act[pl.ds(e, 2), pl.ds(p0 + i // 2, np_), i % 2].reshape(2 * np_ * cols, 3 * C)
                for i in range(4)
            ],
            axis=1,
        )
        o = jnp.dot(lhs, w[...].reshape(12 * C, 2 * C), preferred_element_type=F32)
        o = o.astype(BF16).reshape(2, np_, cols, 2 * C)
        s[pl.ds(e, 2), pl.ds(p0, np_), 0] = o[..., :C]
        s[pl.ds(e, 2), pl.ds(p0, np_), 1] = o[..., C:]

    def temporal(t, s, e, part):
        p0 = part * np_
        lhs = jnp.concatenate(
            [s[e - 2 + i, pl.ds(p0, np_)].reshape(2 * np_ * cols, C) for i in range(4)], axis=1
        )
        return jnp.dot(lhs, t[...].reshape(4 * C, 2 * C), preferred_element_type=F32)

    mid = rows // 2
    pieces = [(1, 1), (rows, 1), (2, 1), (3, mid - 2), (mid + 1, 1), (mid + 2, mid - 2)]
    held = 4
    detour = (3, 4, 5)
    total_at = len(pieces)

    def onward(k, buf, piece):
        r, n = pieces[piece]
        return pltpu.make_async_remote_copy(
            buf.at[pl.ds(frames, 2), pl.ds(r, n)],
            buf.at[pl.ds(0, 2), pl.ds(r, n)],
            y_ssem.at[k, piece],
            y_rsem.at[k, piece],
            device_id={"tm": lax.min(tm + 1, n_tm - 1)},
        )

    def onward_total(k):
        return pltpu.make_async_remote_copy(
            tot_send.at[k],
            tot_recv.at[k],
            y_ssem.at[k, total_at],
            y_rsem.at[k, total_at],
            device_id={"tm": lax.min(tm + 1, n_tm - 1)},
        )

    def at_relay(k, piece):
        r, n = pieces[piece]
        return relay.at[k, :, pl.ds(r, n)]

    def to_relay(k, buf, piece):
        r, n = pieces[piece]
        return pltpu.make_async_remote_copy(
            buf.at[pl.ds(frames, 2), pl.ds(r, n)],
            at_relay(k, piece),
            y_ssem.at[k, piece],
            rl_rsem.at[k, piece],
            device_id={"tm": 0},
        )

    def from_relay(k, buf, piece):
        r, n = pieces[piece]
        return pltpu.make_async_remote_copy(
            at_relay(k, piece),
            buf.at[pl.ds(0, 2), pl.ds(r, n)],
            rl_ssem.at[k, piece],
            y_rsem.at[k, piece],
            device_id={"tm": cross + 1},
        )

    def send_first(k, buf):
        @pl.when(straight)
        def _():
            for piece in range(held):
                onward(k, buf, piece).start()

        @pl.when(crossing)
        def _():
            for piece in detour:
                to_relay(k, buf, piece).start()

    def send_cross(k, buf, some):
        @pl.when(crossing)
        def _():
            for piece in some:
                if piece not in detour:
                    onward(k, buf, piece).start()

    def send_rest(k, buf, packed):
        tot_send[k] = packed

        @pl.when(has_after)
        def _():
            onward_total(k).start()

        @pl.when(straight)
        def _():
            for piece in range(held, len(pieces)):
                onward(k, buf, piece).start()


    def pass_edges(k, buf, copies):
        @pl.when(has_before)
        def _():
            onward(k, buf, 0).wait_recv()
            onward(k, buf, 1).wait_recv()
            send_halo(copies)

    def pass_relay(k, buf, pieces):
        @pl.when(relaying)
        def _():
            for piece in pieces:
                to_relay(k, buf, piece).wait_recv()
                from_relay(k, buf, piece).start()

    def earlier_scales(k, gain):
        onward_total(k).wait_recv()
        packed = tot_recv[k]
        return pair_scales(packed, gain)

    def pair_scales(packed, gain):
        return [scales(unpack(packed, j), unpack(packed, 2 + j), gain) for j in range(2)]

    def activate_pair(src, e, pair, copies):
        fs = [(e + j, *pair[j]) for j in range(2)]
        for f in fs:
            activate_tile(src, *f)
        if copies is not None:
            wait_halo_in(copies)
        activate_halo(src, fs)

    def activate_rows(src, fs, r, n):
        def step(q, _):
            for f in fs:
                activate(src, f[0], q, f[1], f[2])
            return 0

        lax.fori_loop(r, r + n, step, 0)

    def earlier(k, buf, w, s, gain, copies, then):
        @pl.when(has_before)
        def _():
            fs = [(j, *pair) for j, pair in enumerate(earlier_scales(k, gain))]
            onward(k, buf, 2).wait_recv()
            onward(k, buf, 3).wait_recv()
            activate_rows(buf, fs, 1, mid)
            activate_rows(buf, fs, rows, 1)
            wait_halo_in(copies)
            activate_halo(buf, fs)
            onward(k, buf, 4).wait_recv()
            activate_rows(buf, fs, mid + 1, 1)
            spatial(w, s, 0, 0)

        @pl.when(jnp.logical_not(has_before))
        def _():
            s[0] = s[2]
            s[1] = s[2]

        then(0)

        @pl.when(has_before)
        def _():
            fs = [(j, *pair) for j, pair in enumerate(pair_scales(tot_recv[k], gain))]
            onward(k, buf, 5).wait_recv()
            activate_rows(buf, fs, mid + 2, mid - 2)
            spatial(w, s, 0, 1)

        then(1)

    def hidden_part(e, part):
        h = temporal(t1, s1, e, part).astype(BF16)
        own = pl.ds(1 + part * 2 * np_, 2 * np_)
        sums = []
        for j in range(2):
            hj = h[:, j * C : (j + 1) * C]
            hid[e + j, own] = hj.reshape(2 * np_, cols, C)
            sums.append(moments(hj.astype(F32)))
        return [sums[0][0], sums[1][0], sums[0][1], sums[1][1]]

    def hidden(k, e, parts):
        sums = [a + b for a, b in zip(*parts)]
        exchange(k, [pack(sums)])

    def finish(f0, part):
        r = temporal(t2, s2, 2 + f0, part)
        rows_here = 2 * np_
        r0 = part * rows_here
        for j in range(2):
            v = xin[2 + f0 + j, pl.ds(1 + r0, rows_here)].astype(F32)
            total = v + r[:, j * C : (j + 1) * C].reshape(rows_here, cols, C)
            out[f0 + j, pl.ds(r0, rows_here)] = total.astype(BF16)

    sums = []
    for f in range(frames):
        loads[f].wait()

        def add(p, c, f=f):
            x = xin[2 + f, pl.ds(1 + 2 * p, 2)].astype(F32).reshape(-1, 8, C)
            return c[0] + jnp.sum(x, axis=0), c[1] + jnp.sum(x * x, axis=0)

        zero = jnp.zeros((8, C), F32)
        a, b = lax.fori_loop(0, pairs, add, (zero, zero))
        sums.append((jnp.sum(a, axis=0, keepdims=True), jnp.sum(b, axis=0, keepdims=True)))
    packed = [
        pack([sums[f][0], sums[f + 1][0], sums[f][1], sums[f + 1][1]]) for f in range(0, frames, 2)
    ]

    greeted = others + has_before.astype(jnp.int32) + has_after.astype(jnp.int32)
    greeted = greeted + 2 * relaying.astype(jnp.int32)
    greeted = greeted + jnp.logical_or(crossing, relayed).astype(jnp.int32)
    pl.semaphore_wait(barrier, greeted)
    send_first(0, xin)
    exchange(0, packed)
    halo0 = halo_copies(0, xin, 2, frames)
    halo1 = halo_copies(1, hid, 4, 2)
    halo2 = halo_copies(2, hid, 2, 2)
    halo3 = halo_copies(3, xin, 0, 2)
    halo4 = halo_copies(4, hid, 0, 2)
    send_cross(0, xin, (0, 1))
    send_halo(halo0)
    send_cross(0, xin, (2,))

    for load in weight_loads:
        load.wait()
    gain_first = g1[...].reshape(1, C)
    gain_second = g2[...].reshape(1, C)
    pass_edges(0, xin, halo3)
    pass_relay(0, xin, (3,))
    whole01, whole23 = all_sums(0)
    send_rest(0, xin, whole23)
    pass_relay(0, xin, (4,))
    pair01, pair23 = pair_scales(whole01, gain_first), pair_scales(whole23, gain_first)

    activate_pair(xin, 4, pair23, halo0)
    for part in range(PARTS):
        spatial(w1, s1, 4, part)
    pass_relay(0, xin, (5,))
    activate_pair(xin, 2, pair01, None)
    for part in range(PARTS):
        spatial(w1, s1, 2, part)
    hidden(1, 4, [hidden_part(4, part) for part in range(PARTS)])
    send_first(1, hid)
    send_cross(1, hid, (0, 1))
    send_halo(halo1)

    parts = []
    earlier(0, xin, w1, s1, gain_first, halo3, lambda part: parts.append(hidden_part(2, part)))
    hidden(2, 2, parts)
    send_halo(halo2)
    send_cross(1, hid, (2,))

    pass_edges(1, hid, halo4)
    pass_relay(1, hid, (3,))
    (whole23,) = all_sums(1)
    send_rest(1, hid, whole23)
    pass_relay(1, hid, (4,))
    activate_pair(hid, 4, pair_scales(whole23, gain_second), halo1)
    for part in range(PARTS):
        spatial(w2, s2, 4, part)
    pass_relay(1, hid, (5,))

    (whole01,) = all_sums(2)
    activate_pair(hid, 2, pair_scales(whole01, gain_second), halo2)
    for part in range(PARTS):
        spatial(w2, s2, 2, part)
    for part in range(PARTS):
        finish(2, part)
    earlier(1, hid, w2, s2, gain_second, halo4, lambda part: finish(0, part))

    for copies in (halo0, halo1, halo2):
        wait_halo_out(copies)
    for k in range(3):
        whole = st_recv.at[k, pl.ds(0, others), pl.ds(0, sizes(k))]
        pltpu.make_async_copy(whole, whole, st_ssem.at[k]).wait()

    @pl.when(has_before)
    def _():
        for copies in (halo3, halo4):
            wait_halo_out(copies)

    @pl.when(has_after)
    def _():
        for k, buf in ((0, xin), (1, hid)):
            for piece in range(len(pieces)):
                onward(k, buf, piece).wait_send()
            onward_total(k).wait_send()

    for k, buf in ((0, xin), (1, hid)):

        @pl.when(relaying)
        def _():
            for piece in detour:
                from_relay(k, buf, piece).wait_send()


def shards(video, gain1, sp1, tp1, gain2, sp2, tp2):
    frames, rows, cols, channels = video.shape
    n_space = lax.axis_size("space")
    members = rows * n_space * cols * (channels // G)
    hbm = pl.BlockSpec(memory_space=pltpu.HBM)
    inputs = (video, gain1, sp1, tp1, gain2, sp2, tp2)
    call = pl.pallas_call(
        lambda *refs: kernel(float(members), *refs),
        out_shape=pltpu.VMEM(video.shape, BF16),
        in_specs=[hbm] * 7,
        out_specs=pl.BlockSpec(memory_space=pltpu.VMEM),
        scratch_shapes=[
            pltpu.VMEM((frames + 2, rows + 2, cols, C), BF16),
            pltpu.VMEM((frames + 2, rows // 2 + 1, 2, cols, 3 * C), BF16),
            pltpu.VMEM((frames + 2, rows // 2, 2, cols, C), BF16),
            pltpu.VMEM((frames + 2, rows // 2, 2, cols, C), BF16),
            pltpu.VMEM((frames + 2, rows + 2, cols, C), BF16),
            pltpu.VMEM((12, C, 2 * C), BF16),
            pltpu.VMEM((12, C, 2 * C), BF16),
            pltpu.VMEM((4, C, 2 * C), BF16),
            pltpu.VMEM((4, C, 2 * C), BF16),
            pltpu.VMEM((C,), F32),
            pltpu.VMEM((C,), F32),
            pltpu.VMEM((3, 8, C), F32),
            pltpu.VMEM((3, n_space - 1, 8, C), F32),
            pltpu.VMEM((2, 1, C), F32),
            pltpu.VMEM((2, 1, C), F32),
            pltpu.VMEM((2, 2, rows + 2, cols, C), BF16),
            pltpu.SemaphoreType.DMA((frames,)),
            pltpu.SemaphoreType.DMA((10,)),
            pltpu.SemaphoreType.DMA((3,)),
            pltpu.SemaphoreType.DMA((3,)),
            pltpu.SemaphoreType.DMA((5, 2)),
            pltpu.SemaphoreType.DMA((5, 2)),
            pltpu.SemaphoreType.DMA((2, 7)),
            pltpu.SemaphoreType.DMA((2, 7)),
            pltpu.SemaphoreType.DMA((2, 7)),
            pltpu.SemaphoreType.DMA((2, 7)),
        ],
        compiler_params=pltpu.CompilerParams(
            collective_id=0, has_side_effects=True, vmem_limit_bytes=62 * 2**20
        ),
        cost_estimate=pl.CostEstimate(
            flops=4 * 10**9, bytes_accessed=4 * 2**20, transcendentals=10**6
        ),
        name="block",
    )
    return call(*[pltpu.with_memory_space_constraint(x, pltpu.HBM) for x in inputs])


def solution(mesh):
    in_specs = (P("tm", "space", None, None), P(), P(), P(), P(), P(), P())
    out_specs = P("tm", "space", None, None)
    return jax.shard_map(shards, mesh=mesh, in_specs=in_specs, out_specs=out_specs, check_vma=False)
```

```python
import jax
import jax.numpy as jnp
from jax import lax
from jax.experimental import pallas as pl
from jax.experimental.pallas import tpu as pltpu
from jax.sharding import PartitionSpec as P

G = 32
C = 128
norm_eps = 1e-06

F32 = jnp.float32
BF16 = jnp.bfloat16

PARTS = 2


def steps(n_space):
    n_x = n_space // 8

    def hops(step):
        x, z, core = step
        return min(x, n_x - x) + 2 * min(z, 4 - z) + core / 4

    every = [(x, z, core) for x in range(n_x) for z in range(4) for core in range(2)]
    return sorted((s for s in every if s != (0, 0, 0)), key=hops, reverse=True)


def kernel(
    members,
    video, gain1, sp1, tp1, gain2, sp2, tp2, out,
    xin, act, s1, s2, hid, w1, w2, t1, t2, g1, g2, st_send, st_recv, tot_send, tot_recv, relay,
    ld_sem, w_sem, st_ssem, st_rsem, h_ssem, h_rsem, y_ssem, y_rsem, rl_ssem, rl_rsem,
):
    frames, rows, cols, _ = video.shape
    pairs = rows // 2
    n_space, n_tm = lax.axis_size("space"), lax.axis_size("tm")
    space, tm = lax.axis_index("space"), lax.axis_index("tm")
    has_up, has_down = space > 0, space < n_space - 1
    has_before, has_after = tm > 0, tm < n_tm - 1
    cross = n_tm // 2 - 1
    crossing = tm == cross
    straight = jnp.logical_and(has_after, jnp.logical_not(crossing))
    relaying = tm == 0
    relayed = tm == cross + 1
    others = n_space - 1
    apart = steps(n_space)

    def tile(place):
        x, z, core = apart[place]
        across = lax.rem(space // 8 + x, n_space // 8)
        along = lax.rem(lax.rem(space // 2, 4) + z, 4)
        return across * 8 + along * 2 + lax.rem(space + core, 2)

    barrier = pltpu.get_barrier_semaphore()

    for place in range(others):
        pl.semaphore_signal(barrier, 1, device_id={"space": tile(place)})

    @pl.when(has_before)
    def _():
        pl.semaphore_signal(barrier, 1, device_id={"tm": tm - 1})

    @pl.when(has_after)
    def _():
        pl.semaphore_signal(barrier, 1, device_id={"tm": tm + 1})

    @pl.when(relaying)
    def _():
        pl.semaphore_signal(barrier, 1, device_id={"tm": cross})
        pl.semaphore_signal(barrier, 1, device_id={"tm": cross + 1})

    @pl.when(jnp.logical_or(crossing, relayed))
    def _():
        pl.semaphore_signal(barrier, 1, device_id={"tm": 0})

    loads = [
        pltpu.make_async_copy(video.at[f], xin.at[2 + f, pl.ds(1, rows)], ld_sem.at[f])
        for f in range(frames)
    ]
    for load in loads:
        load.start()
    weight_loads = [
        pltpu.make_async_copy(gain1, g1, w_sem.at[0]),
        pltpu.make_async_copy(sp1, w1.at[pl.ds(0, 9), :, pl.ds(0, C)], w_sem.at[1]),
        pltpu.make_async_copy(sp1, w1.at[pl.ds(3, 9), :, pl.ds(C, C)], w_sem.at[2]),
        pltpu.make_async_copy(tp1, t1.at[pl.ds(0, 3), :, pl.ds(0, C)], w_sem.at[3]),
        pltpu.make_async_copy(tp1, t1.at[pl.ds(1, 3), :, pl.ds(C, C)], w_sem.at[4]),
        pltpu.make_async_copy(gain2, g2, w_sem.at[5]),
        pltpu.make_async_copy(sp2, w2.at[pl.ds(0, 9), :, pl.ds(0, C)], w_sem.at[6]),
        pltpu.make_async_copy(sp2, w2.at[pl.ds(3, 9), :, pl.ds(C, C)], w_sem.at[7]),
        pltpu.make_async_copy(tp2, t2.at[pl.ds(0, 3), :, pl.ds(0, C)], w_sem.at[8]),
        pltpu.make_async_copy(tp2, t2.at[pl.ds(1, 3), :, pl.ds(C, C)], w_sem.at[9]),
    ]
    for load in weight_loads:
        load.start()
    for w in (w1, w2):
        w[pl.ds(9, 3), :, pl.ds(0, C)] = jnp.zeros((3, C, C), BF16)
        w[pl.ds(0, 3), :, pl.ds(C, C)] = jnp.zeros((3, C, C), BF16)
    for t in (t1, t2):
        t[pl.ds(3, 1), :, pl.ds(0, C)] = jnp.zeros((1, C, C), BF16)
        t[pl.ds(0, 1), :, pl.ds(C, C)] = jnp.zeros((1, C, C), BF16)

    def moments(x):
        x = x.reshape(-1, 8, C)
        return (
            jnp.sum(jnp.sum(x, axis=0), axis=0, keepdims=True),
            jnp.sum(jnp.sum(x * x, axis=0), axis=0, keepdims=True),
        )

    group = C // G
    lane = lax.broadcasted_iota(jnp.int32, (1, C), 1)

    def over_group(x):
        step = 1
        while step < group:
            low = lax.rem(lane, 2 * step) < step
            x = x + jnp.where(low, pltpu.roll(x, C - step, 1), pltpu.roll(x, step, 1))
            step *= 2
        return x

    def pack(rows_in):
        packed = jnp.zeros((1, C), F32)
        for i, x in enumerate(rows_in):
            packed = jnp.where(lax.rem(lane, group) == i, over_group(x), packed)
        return packed

    def unpack(packed, i):
        return over_group(jnp.where(lax.rem(lane, group) == i, packed, 0.0))

    def sizes(k):
        return 2 if k == 0 else 1

    def exchange(k, packed):
        n = sizes(k)
        for i, x in enumerate(packed):
            st_send[k, pl.ds(i, 1)] = x

        for place in range(others):
            pltpu.make_async_remote_copy(
                st_send.at[k, pl.ds(0, n)],
                st_recv.at[k, place, pl.ds(0, n)],
                st_ssem.at[k],
                st_rsem.at[k],
                device_id={"space": tile(place)},
            ).start()

    def all_sums(k):
        n = sizes(k)
        whole = st_recv.at[k, pl.ds(0, others), pl.ds(0, n)]
        pltpu.make_async_copy(whole, whole, st_rsem.at[k]).wait()
        return [
            st_send[k, pl.ds(i, 1)] + jnp.sum(st_recv[k, :, pl.ds(i, 1)], axis=0) for i in range(n)
        ]

    def scales(total, square, gain):
        center = total / members
        inverse = lax.rsqrt(square / members - center * center + norm_eps)
        return center, inverse * gain * 0.5

    first_col = lax.broadcasted_iota(jnp.int32, (cols, C), 0) == 0
    last_col = lax.broadcasted_iota(jnp.int32, (cols, C), 0) == cols - 1

    def activate(src, f, q, center, half):
        h = (src[f, q].astype(F32) - center) * half
        a = h * (1.0 + jnp.tanh(h))
        left = jnp.where(first_col, 0.0, pltpu.roll(a, 1, 0))
        right = jnp.where(last_col, 0.0, pltpu.roll(a, cols - 1, 0))
        act[f, q // 2, q % 2, :, pl.ds(0, C)] = left.astype(BF16)
        act[f, q // 2, q % 2, :, pl.ds(C, C)] = a.astype(BF16)
        act[f, q // 2, q % 2, :, pl.ds(2 * C, C)] = right.astype(BF16)

    def activate_tile(src, f, center, half):
        def step(p, _):
            for o in (1, 2):
                activate(src, f, 2 * p + o, center, half)
            return 0

        lax.fori_loop(0, pairs, step, 0)

    def halo_copies(k, buf, e, n):
        up = pltpu.make_async_remote_copy(
            buf.at[pl.ds(e, n), 1],
            buf.at[pl.ds(e, n), rows + 1],
            h_ssem.at[k, 0],
            h_rsem.at[k, 0],
            device_id={"space": lax.max(space - 1, 0)},
        )
        down = pltpu.make_async_remote_copy(
            buf.at[pl.ds(e, n), rows],
            buf.at[pl.ds(e, n), 0],
            h_ssem.at[k, 1],
            h_rsem.at[k, 1],
            device_id={"space": lax.min(space + 1, n_space - 1)},
        )
        return up, down

    def send_halo(copies):
        up, down = copies

        @pl.when(has_up)
        def _():
            up.start()

        @pl.when(has_down)
        def _():
            down.start()

    def wait_halo_in(copies):
        up, down = copies

        @pl.when(has_down)
        def _():
            up.wait_recv()

        @pl.when(has_up)
        def _():
            down.wait_recv()

    def wait_halo_out(copies):
        up, down = copies

        @pl.when(has_up)
        def _():
            up.wait_send()

        @pl.when(has_down)
        def _():
            down.wait_send()

    def activate_halo(src, fs):
        for present, q in ((has_up, 0), (has_down, rows + 1)):

            @pl.when(present)
            def _():
                for f, center, half in fs:
                    activate(src, f, q, center, half)

            @pl.when(jnp.logical_not(present))
            def _():
                for f, _c, _h in fs:
                    act[f, q // 2, q % 2] = jnp.zeros((cols, 3 * C), BF16)

    np_ = pairs // PARTS

    def spatial(w, s, e, part):
        p0 = part * np_
        lhs = jnp.concatenate(
            [
                act[pl.ds(e, 2), pl.ds(p0 + i // 2, np_), i % 2].reshape(2 * np_ * cols, 3 * C)
                for i in range(4)
            ],
            axis=1,
        )
        o = jnp.dot(lhs, w[...].reshape(12 * C, 2 * C), preferred_element_type=F32)
        o = o.astype(BF16).reshape(2, np_, cols, 2 * C)
        s[pl.ds(e, 2), pl.ds(p0, np_), 0] = o[..., :C]
        s[pl.ds(e, 2), pl.ds(p0, np_), 1] = o[..., C:]

    def temporal(t, s, e, part):
        p0 = part * np_
        lhs = jnp.concatenate(
            [s[e - 2 + i, pl.ds(p0, np_)].reshape(2 * np_ * cols, C) for i in range(4)], axis=1
        )
        return jnp.dot(lhs, t[...].reshape(4 * C, 2 * C), preferred_element_type=F32)

    mid = rows // 2
    pieces = [(1, 1), (rows, 1), (2, 1), (3, mid - 2), (mid + 1, 1), (mid + 2, mid - 2)]
    held = 4
    detour = (3, 4, 5)
    total_at = len(pieces)

    def onward(k, buf, piece):
        r, n = pieces[piece]
        return pltpu.make_async_remote_copy(
            buf.at[pl.ds(frames, 2), pl.ds(r, n)],
            buf.at[pl.ds(0, 2), pl.ds(r, n)],
            y_ssem.at[k, piece],
            y_rsem.at[k, piece],
            device_id={"tm": lax.min(tm + 1, n_tm - 1)},
        )

    def onward_total(k):
        return pltpu.make_async_remote_copy(
            tot_send.at[k],
            tot_recv.at[k],
            y_ssem.at[k, total_at],
            y_rsem.at[k, total_at],
            device_id={"tm": lax.min(tm + 1, n_tm - 1)},
        )

    def at_relay(k, piece):
        r, n = pieces[piece]
        return relay.at[k, :, pl.ds(r, n)]

    def to_relay(k, buf, piece):
        r, n = pieces[piece]
        return pltpu.make_async_remote_copy(
            buf.at[pl.ds(frames, 2), pl.ds(r, n)],
            at_relay(k, piece),
            y_ssem.at[k, piece],
            rl_rsem.at[k, piece],
            device_id={"tm": 0},
        )

    def from_relay(k, buf, piece):
        r, n = pieces[piece]
        return pltpu.make_async_remote_copy(
            at_relay(k, piece),
            buf.at[pl.ds(0, 2), pl.ds(r, n)],
            rl_ssem.at[k, piece],
            y_rsem.at[k, piece],
            device_id={"tm": cross + 1},
        )

    def send_first(k, buf):
        @pl.when(straight)
        def _():
            for piece in range(held):
                onward(k, buf, piece).start()

        @pl.when(crossing)
        def _():
            for piece in detour:
                to_relay(k, buf, piece).start()

    def send_cross(k, buf, some):
        @pl.when(crossing)
        def _():
            for piece in some:
                if piece not in detour:
                    onward(k, buf, piece).start()

    def send_rest(k, buf, packed):
        tot_send[k] = packed

        @pl.when(has_after)
        def _():
            onward_total(k).start()

        @pl.when(straight)
        def _():
            for piece in range(held, len(pieces)):
                onward(k, buf, piece).start()


    unrelayed = jnp.logical_and(has_before, jnp.logical_not(relayed))

    def pass_edges(k, buf, copies, when):
        @pl.when(when)
        def _():
            onward(k, buf, 0).wait_recv()
            onward(k, buf, 1).wait_recv()
            send_halo(copies)

    def pass_relay(k, buf, pieces):
        @pl.when(relaying)
        def _():
            for piece in pieces:
                to_relay(k, buf, piece).wait_recv()
                from_relay(k, buf, piece).start()

    def earlier_scales(k, gain):
        onward_total(k).wait_recv()
        packed = tot_recv[k]
        return pair_scales(packed, gain)

    def pair_scales(packed, gain):
        return [scales(unpack(packed, j), unpack(packed, 2 + j), gain) for j in range(2)]

    def activate_pair(src, e, pair, copies):
        fs = [(e + j, *pair[j]) for j in range(2)]
        for f in fs:
            activate_tile(src, *f)
        wait_halo_in(copies)
        activate_halo(src, fs)

    def activate_rows(src, fs, r, n):
        def step(q, _):
            for f in fs:
                activate(src, f[0], q, f[1], f[2])
            return 0

        lax.fori_loop(r, r + n, step, 0)

    def earlier(k, buf, w, s, gain, copies, then):
        @pl.when(has_before)
        def _():
            fs = [(j, *pair) for j, pair in enumerate(earlier_scales(k, gain))]
            onward(k, buf, 2).wait_recv()
            onward(k, buf, 3).wait_recv()
            activate_rows(buf, fs, 1, mid)
            activate_rows(buf, fs, rows, 1)
            wait_halo_in(copies)
            activate_halo(buf, fs)
            onward(k, buf, 4).wait_recv()
            activate_rows(buf, fs, mid + 1, 1)
            spatial(w, s, 0, 0)

        @pl.when(jnp.logical_not(has_before))
        def _():
            s[0] = s[2]
            s[1] = s[2]

        then(0)

        @pl.when(has_before)
        def _():
            fs = [(j, *pair) for j, pair in enumerate(pair_scales(tot_recv[k], gain))]
            onward(k, buf, 5).wait_recv()
            activate_rows(buf, fs, mid + 2, mid - 2)
            spatial(w, s, 0, 1)

        then(1)

    def hidden_part(e, part):
        h = temporal(t1, s1, e, part).astype(BF16)
        own = pl.ds(1 + part * 2 * np_, 2 * np_)
        sums = []
        for j in range(2):
            hj = h[:, j * C : (j + 1) * C]
            hid[e + j, own] = hj.reshape(2 * np_, cols, C)
            sums.append(moments(hj.astype(F32)))
        return [sums[0][0], sums[1][0], sums[0][1], sums[1][1]]

    def hidden(k, e, parts):
        sums = [a + b for a, b in zip(*parts)]
        exchange(k, [pack(sums)])

    def finish(f0, part):
        r = temporal(t2, s2, 2 + f0, part)
        rows_here = 2 * np_
        r0 = part * rows_here
        for j in range(2):
            v = xin[2 + f0 + j, pl.ds(1 + r0, rows_here)].astype(F32)
            total = v + r[:, j * C : (j + 1) * C].reshape(rows_here, cols, C)
            out[f0 + j, pl.ds(r0, rows_here)] = total.astype(BF16)

    sums = []
    for f in range(frames):
        loads[f].wait()

        def add(p, c, f=f):
            x = xin[2 + f, pl.ds(1 + 2 * p, 2)].astype(F32).reshape(-1, 8, C)
            return c[0] + jnp.sum(x, axis=0), c[1] + jnp.sum(x * x, axis=0)

        zero = jnp.zeros((8, C), F32)
        a, b = lax.fori_loop(0, pairs, add, (zero, zero))
        sums.append((jnp.sum(a, axis=0, keepdims=True), jnp.sum(b, axis=0, keepdims=True)))
    packed = [
        pack([sums[f][0], sums[f + 1][0], sums[f][1], sums[f + 1][1]]) for f in range(0, frames, 2)
    ]

    greeted = others + has_before.astype(jnp.int32) + has_after.astype(jnp.int32)
    greeted = greeted + 2 * relaying.astype(jnp.int32)
    greeted = greeted + jnp.logical_or(crossing, relayed).astype(jnp.int32)
    pl.semaphore_wait(barrier, greeted)
    send_first(0, xin)
    exchange(0, packed)
    halo0 = halo_copies(0, xin, 4, 2)
    halo5 = halo_copies(5, xin, 2, 2)
    halo1 = halo_copies(1, hid, 4, 2)
    halo2 = halo_copies(2, hid, 2, 2)
    halo3 = halo_copies(3, xin, 0, 2)
    halo4 = halo_copies(4, hid, 0, 2)
    send_halo(halo0)
    send_halo(halo5)
    send_cross(0, xin, (0, 1, 2))

    for load in weight_loads:
        load.wait()
    gain_first = g1[...].reshape(1, C)
    gain_second = g2[...].reshape(1, C)
    pass_edges(0, xin, halo3, unrelayed)
    pass_relay(0, xin, (3,))
    whole01, whole23 = all_sums(0)
    send_rest(0, xin, whole23)
    pass_relay(0, xin, (4,))
    pair01, pair23 = pair_scales(whole01, gain_first), pair_scales(whole23, gain_first)

    activate_pair(xin, 4, pair23, halo0)
    for part in range(PARTS):
        spatial(w1, s1, 4, part)
    pass_relay(0, xin, (5,))
    pass_edges(0, xin, halo3, relayed)
    activate_pair(xin, 2, pair01, halo5)
    for part in range(PARTS):
        spatial(w1, s1, 2, part)
    hidden(1, 4, [hidden_part(4, part) for part in range(PARTS)])
    send_first(1, hid)
    send_halo(halo1)
    send_cross(1, hid, (0, 1))

    parts = []
    earlier(0, xin, w1, s1, gain_first, halo3, lambda part: parts.append(hidden_part(2, part)))
    hidden(2, 2, parts)
    send_halo(halo2)

    pass_edges(1, hid, halo4, unrelayed)
    pass_relay(1, hid, (3,))
    (whole23,) = all_sums(1)
    send_rest(1, hid, whole23)
    send_cross(1, hid, (2,))
    pass_relay(1, hid, (4,))
    activate_pair(hid, 4, pair_scales(whole23, gain_second), halo1)
    for part in range(PARTS):
        spatial(w2, s2, 4, part)
    pass_relay(1, hid, (5,))
    pass_edges(1, hid, halo4, relayed)

    (whole01,) = all_sums(2)
    activate_pair(hid, 2, pair_scales(whole01, gain_second), halo2)
    for part in range(PARTS):
        spatial(w2, s2, 2, part)
    for part in range(PARTS):
        finish(2, part)
    earlier(1, hid, w2, s2, gain_second, halo4, lambda part: finish(0, part))

    for copies in (halo0, halo1, halo2, halo5):
        wait_halo_out(copies)
    for k in range(3):
        whole = st_recv.at[k, pl.ds(0, others), pl.ds(0, sizes(k))]
        pltpu.make_async_copy(whole, whole, st_ssem.at[k]).wait()

    @pl.when(has_before)
    def _():
        for copies in (halo3, halo4):
            wait_halo_out(copies)

    @pl.when(has_after)
    def _():
        for k, buf in ((0, xin), (1, hid)):
            for piece in range(len(pieces)):
                onward(k, buf, piece).wait_send()
            onward_total(k).wait_send()

    for k, buf in ((0, xin), (1, hid)):

        @pl.when(relaying)
        def _():
            for piece in detour:
                from_relay(k, buf, piece).wait_send()


def shards(video, gain1, sp1, tp1, gain2, sp2, tp2):
    frames, rows, cols, channels = video.shape
    n_space = lax.axis_size("space")
    members = rows * n_space * cols * (channels // G)
    hbm = pl.BlockSpec(memory_space=pltpu.HBM)
    inputs = (video, gain1, sp1, tp1, gain2, sp2, tp2)
    call = pl.pallas_call(
        lambda *refs: kernel(float(members), *refs),
        out_shape=pltpu.VMEM(video.shape, BF16),
        in_specs=[hbm] * 7,
        out_specs=pl.BlockSpec(memory_space=pltpu.VMEM),
        scratch_shapes=[
            pltpu.VMEM((frames + 2, rows + 2, cols, C), BF16),
            pltpu.VMEM((frames + 2, rows // 2 + 1, 2, cols, 3 * C), BF16),
            pltpu.VMEM((frames + 2, rows // 2, 2, cols, C), BF16),
            pltpu.VMEM((frames + 2, rows // 2, 2, cols, C), BF16),
            pltpu.VMEM((frames + 2, rows + 2, cols, C), BF16),
            pltpu.VMEM((12, C, 2 * C), BF16),
            pltpu.VMEM((12, C, 2 * C), BF16),
            pltpu.VMEM((4, C, 2 * C), BF16),
            pltpu.VMEM((4, C, 2 * C), BF16),
            pltpu.VMEM((C,), F32),
            pltpu.VMEM((C,), F32),
            pltpu.VMEM((3, 8, C), F32),
            pltpu.VMEM((3, n_space - 1, 8, C), F32),
            pltpu.VMEM((2, 1, C), F32),
            pltpu.VMEM((2, 1, C), F32),
            pltpu.VMEM((2, 2, rows + 2, cols, C), BF16),
            pltpu.SemaphoreType.DMA((frames,)),
            pltpu.SemaphoreType.DMA((10,)),
            pltpu.SemaphoreType.DMA((3,)),
            pltpu.SemaphoreType.DMA((3,)),
            pltpu.SemaphoreType.DMA((6, 2)),
            pltpu.SemaphoreType.DMA((6, 2)),
            pltpu.SemaphoreType.DMA((2, 7)),
            pltpu.SemaphoreType.DMA((2, 7)),
            pltpu.SemaphoreType.DMA((2, 7)),
            pltpu.SemaphoreType.DMA((2, 7)),
        ],
        compiler_params=pltpu.CompilerParams(
            collective_id=0, has_side_effects=True, vmem_limit_bytes=62 * 2**20
        ),
        cost_estimate=pl.CostEstimate(
            flops=4 * 10**9, bytes_accessed=4 * 2**20, transcendentals=10**6
        ),
        name="block",
    )
    return call(*[pltpu.with_memory_space_constraint(x, pltpu.HBM) for x in inputs])


def solution(mesh):
    in_specs = (P("tm", "space", None, None), P(), P(), P(), P(), P(), P())
    out_specs = P("tm", "space", None, None)
    return jax.shard_map(shards, mesh=mesh, in_specs=in_specs, out_specs=out_specs, check_vma=False)
```

```python
import jax
import jax.numpy as jnp
from jax import lax
from jax.experimental import pallas as pl
from jax.experimental.pallas import tpu as pltpu
from jax.sharding import PartitionSpec as P

G = 32
C = 128
norm_eps = 1e-06

F32 = jnp.float32
BF16 = jnp.bfloat16

PARTS = 2


def steps(n_space):
    n_x = n_space // 8

    def hops(step):
        x, z, core = step
        return min(x, n_x - x) + 2 * min(z, 4 - z) + core / 4

    every = [(x, z, core) for x in range(n_x) for z in range(4) for core in range(2)]
    return sorted((s for s in every if s != (0, 0, 0)), key=hops, reverse=True)


def kernel(
    members,
    video, gain1, sp1, tp1, gain2, sp2, tp2, out,
    xin, act, s1, s2, hid, w1, w2, t1, t2, g1, g2, st_send, st_recv, tot_send, tot_recv, relay,
    ld_sem, w_sem, st_ssem, st_rsem, h_ssem, h_rsem, y_ssem, y_rsem, rl_ssem, rl_rsem,
):
    frames, rows, cols, _ = video.shape
    pairs = rows // 2
    n_space, n_tm = lax.axis_size("space"), lax.axis_size("tm")
    space, tm = lax.axis_index("space"), lax.axis_index("tm")
    has_up, has_down = space > 0, space < n_space - 1
    has_before, has_after = tm > 0, tm < n_tm - 1
    cross = n_tm // 2 - 1
    crossing = tm == cross
    straight = jnp.logical_and(has_after, jnp.logical_not(crossing))
    relaying = tm == 0
    relayed = tm == cross + 1
    others = n_space - 1
    apart = steps(n_space)

    def tile(place):
        x, z, core = apart[place]
        across = lax.rem(space // 8 + x, n_space // 8)
        along = lax.rem(lax.rem(space // 2, 4) + z, 4)
        return across * 8 + along * 2 + lax.rem(space + core, 2)

    barrier = pltpu.get_barrier_semaphore()

    for place in range(others):
        pl.semaphore_signal(barrier, 1, device_id={"space": tile(place)})

    @pl.when(has_before)
    def _():
        pl.semaphore_signal(barrier, 1, device_id={"tm": tm - 1})

    @pl.when(has_after)
    def _():
        pl.semaphore_signal(barrier, 1, device_id={"tm": tm + 1})

    @pl.when(relaying)
    def _():
        pl.semaphore_signal(barrier, 1, device_id={"tm": cross})
        pl.semaphore_signal(barrier, 1, device_id={"tm": cross + 1})

    @pl.when(jnp.logical_or(crossing, relayed))
    def _():
        pl.semaphore_signal(barrier, 1, device_id={"tm": 0})

    loads = [
        pltpu.make_async_copy(video.at[f], xin.at[2 + f, pl.ds(1, rows)], ld_sem.at[f])
        for f in range(frames)
    ]
    for load in loads:
        load.start()
    weight_loads = [
        pltpu.make_async_copy(gain1, g1, w_sem.at[0]),
        pltpu.make_async_copy(sp1, w1.at[pl.ds(0, 9), :, pl.ds(0, C)], w_sem.at[1]),
        pltpu.make_async_copy(sp1, w1.at[pl.ds(3, 9), :, pl.ds(C, C)], w_sem.at[2]),
        pltpu.make_async_copy(tp1, t1.at[pl.ds(0, 3), :, pl.ds(0, C)], w_sem.at[3]),
        pltpu.make_async_copy(tp1, t1.at[pl.ds(1, 3), :, pl.ds(C, C)], w_sem.at[4]),
        pltpu.make_async_copy(gain2, g2, w_sem.at[5]),
        pltpu.make_async_copy(sp2, w2.at[pl.ds(0, 9), :, pl.ds(0, C)], w_sem.at[6]),
        pltpu.make_async_copy(sp2, w2.at[pl.ds(3, 9), :, pl.ds(C, C)], w_sem.at[7]),
        pltpu.make_async_copy(tp2, t2.at[pl.ds(0, 3), :, pl.ds(0, C)], w_sem.at[8]),
        pltpu.make_async_copy(tp2, t2.at[pl.ds(1, 3), :, pl.ds(C, C)], w_sem.at[9]),
    ]
    for load in weight_loads:
        load.start()
    for w in (w1, w2):
        w[pl.ds(9, 3), :, pl.ds(0, C)] = jnp.zeros((3, C, C), BF16)
        w[pl.ds(0, 3), :, pl.ds(C, C)] = jnp.zeros((3, C, C), BF16)
    for t in (t1, t2):
        t[pl.ds(3, 1), :, pl.ds(0, C)] = jnp.zeros((1, C, C), BF16)
        t[pl.ds(0, 1), :, pl.ds(C, C)] = jnp.zeros((1, C, C), BF16)

    def moments(x):
        x = x.reshape(-1, 8, C)
        return (
            jnp.sum(jnp.sum(x, axis=0), axis=0, keepdims=True),
            jnp.sum(jnp.sum(x * x, axis=0), axis=0, keepdims=True),
        )

    group = C // G
    lane = lax.broadcasted_iota(jnp.int32, (1, C), 1)

    def over_group(x):
        step = 1
        while step < group:
            low = lax.rem(lane, 2 * step) < step
            x = x + jnp.where(low, pltpu.roll(x, C - step, 1), pltpu.roll(x, step, 1))
            step *= 2
        return x

    def pack(rows_in):
        packed = jnp.zeros((1, C), F32)
        for i, x in enumerate(rows_in):
            packed = jnp.where(lax.rem(lane, group) == i, over_group(x), packed)
        return packed

    def unpack(packed, i):
        return over_group(jnp.where(lax.rem(lane, group) == i, packed, 0.0))

    def sizes(k):
        return 2 if k == 0 else 1

    def exchange(k, packed):
        n = sizes(k)
        for i, x in enumerate(packed):
            st_send[k, pl.ds(i, 1)] = x

        for place in range(others):
            pltpu.make_async_remote_copy(
                st_send.at[k, pl.ds(0, n)],
                st_recv.at[k, place, pl.ds(0, n)],
                st_ssem.at[k],
                st_rsem.at[k],
                device_id={"space": tile(place)},
            ).start()

    def all_sums(k):
        n = sizes(k)
        whole = st_recv.at[k, pl.ds(0, others), pl.ds(0, n)]
        pltpu.make_async_copy(whole, whole, st_rsem.at[k]).wait()
        return [
            st_send[k, pl.ds(i, 1)] + jnp.sum(st_recv[k, :, pl.ds(i, 1)], axis=0) for i in range(n)
        ]

    def scales(total, square, gain):
        center = total / members
        inverse = lax.rsqrt(square / members - center * center + norm_eps)
        return center, inverse * gain * 0.5

    first_col = lax.broadcasted_iota(jnp.int32, (cols, C), 0) == 0
    last_col = lax.broadcasted_iota(jnp.int32, (cols, C), 0) == cols - 1

    def activate(src, f, q, center, half):
        h = (src[f, q].astype(F32) - center) * half
        a = h * (1.0 + jnp.tanh(h))
        left = jnp.where(first_col, 0.0, pltpu.roll(a, 1, 0))
        right = jnp.where(last_col, 0.0, pltpu.roll(a, cols - 1, 0))
        act[f, q // 2, q % 2, :, pl.ds(0, C)] = left.astype(BF16)
        act[f, q // 2, q % 2, :, pl.ds(C, C)] = a.astype(BF16)
        act[f, q // 2, q % 2, :, pl.ds(2 * C, C)] = right.astype(BF16)

    def activate_tile(src, f, center, half):
        def step(p, _):
            for o in (1, 2):
                activate(src, f, 2 * p + o, center, half)
            return 0

        lax.fori_loop(0, pairs, step, 0)

    def halo_copies(k, buf, e, n):
        up = pltpu.make_async_remote_copy(
            buf.at[pl.ds(e, n), 1],
            buf.at[pl.ds(e, n), rows + 1],
            h_ssem.at[k, 0],
            h_rsem.at[k, 0],
            device_id={"space": lax.max(space - 1, 0)},
        )
        down = pltpu.make_async_remote_copy(
            buf.at[pl.ds(e, n), rows],
            buf.at[pl.ds(e, n), 0],
            h_ssem.at[k, 1],
            h_rsem.at[k, 1],
            device_id={"space": lax.min(space + 1, n_space - 1)},
        )
        return up, down

    def send_halo(copies):
        up, down = copies

        @pl.when(has_up)
        def _():
            up.start()

        @pl.when(has_down)
        def _():
            down.start()

    def wait_halo_in(copies):
        up, down = copies

        @pl.when(has_down)
        def _():
            up.wait_recv()

        @pl.when(has_up)
        def _():
            down.wait_recv()

    def wait_halo_out(copies):
        up, down = copies

        @pl.when(has_up)
        def _():
            up.wait_send()

        @pl.when(has_down)
        def _():
            down.wait_send()

    def activate_halo(src, fs):
        for present, q in ((has_up, 0), (has_down, rows + 1)):

            @pl.when(present)
            def _():
                for f, center, half in fs:
                    activate(src, f, q, center, half)

            @pl.when(jnp.logical_not(present))
            def _():
                for f, _c, _h in fs:
                    act[f, q // 2, q % 2] = jnp.zeros((cols, 3 * C), BF16)

    np_ = pairs // PARTS

    def spatial(w, s, e, part):
        p0 = part * np_
        lhs = jnp.concatenate(
            [
                act[pl.ds(e, 2), pl.ds(p0 + i // 2, np_), i % 2].reshape(2 * np_ * cols, 3 * C)
                for i in range(4)
            ],
            axis=1,
        )
        o = jnp.dot(lhs, w[...].reshape(12 * C, 2 * C), preferred_element_type=F32)
        o = o.astype(BF16).reshape(2, np_, cols, 2 * C)
        s[pl.ds(e, 2), pl.ds(p0, np_), 0] = o[..., :C]
        s[pl.ds(e, 2), pl.ds(p0, np_), 1] = o[..., C:]

    def temporal(t, s, e, part):
        p0 = part * np_
        lhs = jnp.concatenate(
            [s[e - 2 + i, pl.ds(p0, np_)].reshape(2 * np_ * cols, C) for i in range(4)], axis=1
        )
        return jnp.dot(lhs, t[...].reshape(4 * C, 2 * C), preferred_element_type=F32)

    mid = rows // 2
    pieces = [(1, 1), (rows, 1), (2, 1), (3, mid - 2), (mid + 1, 1), (mid + 2, mid - 2)]
    held = 4
    detour = (3, 4, 5)
    total_at = len(pieces)

    def onward(k, buf, piece):
        r, n = pieces[piece]
        return pltpu.make_async_remote_copy(
            buf.at[pl.ds(frames, 2), pl.ds(r, n)],
            buf.at[pl.ds(0, 2), pl.ds(r, n)],
            y_ssem.at[k, piece],
            y_rsem.at[k, piece],
            device_id={"tm": lax.min(tm + 1, n_tm - 1)},
        )

    def onward_total(k):
        return pltpu.make_async_remote_copy(
            tot_send.at[k],
            tot_recv.at[k],
            y_ssem.at[k, total_at],
            y_rsem.at[k, total_at],
            device_id={"tm": lax.min(tm + 1, n_tm - 1)},
        )

    def at_relay(k, piece):
        r, n = pieces[piece]
        return relay.at[k, :, pl.ds(r, n)]

    def to_relay(k, buf, piece):
        r, n = pieces[piece]
        return pltpu.make_async_remote_copy(
            buf.at[pl.ds(frames, 2), pl.ds(r, n)],
            at_relay(k, piece),
            y_ssem.at[k, piece],
            rl_rsem.at[k, piece],
            device_id={"tm": 0},
        )

    def from_relay(k, buf, piece):
        r, n = pieces[piece]
        return pltpu.make_async_remote_copy(
            at_relay(k, piece),
            buf.at[pl.ds(0, 2), pl.ds(r, n)],
            rl_ssem.at[k, piece],
            y_rsem.at[k, piece],
            device_id={"tm": cross + 1},
        )

    def send_first(k, buf):
        @pl.when(straight)
        def _():
            for piece in range(held):
                onward(k, buf, piece).start()

        @pl.when(crossing)
        def _():
            for piece in detour:
                to_relay(k, buf, piece).start()

    def send_cross(k, buf, some):
        @pl.when(crossing)
        def _():
            for piece in some:
                if piece not in detour:
                    onward(k, buf, piece).start()

    def send_rest(k, buf, packed):
        tot_send[k] = packed

        @pl.when(has_after)
        def _():
            onward_total(k).start()

        @pl.when(straight)
        def _():
            for piece in range(held, len(pieces)):
                onward(k, buf, piece).start()


    unrelayed = jnp.logical_and(has_before, jnp.logical_not(relayed))

    def pass_edges(k, buf, copies, when):
        @pl.when(when)
        def _():
            onward(k, buf, 0).wait_recv()
            onward(k, buf, 1).wait_recv()
            send_halo(copies)

    def pass_relay(k, buf, pieces):
        @pl.when(relaying)
        def _():
            for piece in pieces:
                to_relay(k, buf, piece).wait_recv()
                from_relay(k, buf, piece).start()

    def earlier_scales(k, gain):
        onward_total(k).wait_recv()
        packed = tot_recv[k]
        return pair_scales(packed, gain)

    def pair_scales(packed, gain):
        return [scales(unpack(packed, j), unpack(packed, 2 + j), gain) for j in range(2)]

    def activate_pair(src, e, pair, copies):
        fs = [(e + j, *pair[j]) for j in range(2)]
        for f in fs:
            activate_tile(src, *f)
        wait_halo_in(copies)
        activate_halo(src, fs)

    def activate_rows(src, fs, r, n):
        def step(q, _):
            for f in fs:
                activate(src, f[0], q, f[1], f[2])
            return 0

        lax.fori_loop(r, r + n, step, 0)

    def earlier(k, buf, w, s, gain, copies, then):
        @pl.when(has_before)
        def _():
            fs = [(j, *pair) for j, pair in enumerate(earlier_scales(k, gain))]
            onward(k, buf, 2).wait_recv()
            onward(k, buf, 3).wait_recv()
            activate_rows(buf, fs, 1, mid)
            activate_rows(buf, fs, rows, 1)
            wait_halo_in(copies)
            activate_halo(buf, fs)
            onward(k, buf, 4).wait_recv()
            activate_rows(buf, fs, mid + 1, 1)
            spatial(w, s, 0, 0)

        @pl.when(jnp.logical_not(has_before))
        def _():
            s[0] = s[2]
            s[1] = s[2]

        then(0)

        @pl.when(has_before)
        def _():
            fs = [(j, *pair) for j, pair in enumerate(pair_scales(tot_recv[k], gain))]
            onward(k, buf, 5).wait_recv()
            activate_rows(buf, fs, mid + 2, mid - 2)
            spatial(w, s, 0, 1)

        then(1)

    def hidden_part(e, part):
        h = temporal(t1, s1, e, part).astype(BF16)
        own = pl.ds(1 + part * 2 * np_, 2 * np_)
        sums = []
        for j in range(2):
            hj = h[:, j * C : (j + 1) * C]
            hid[e + j, own] = hj.reshape(2 * np_, cols, C)
            sums.append(moments(hj.astype(F32)))
        return [sums[0][0], sums[1][0], sums[0][1], sums[1][1]]

    def hidden(k, e, parts):
        sums = [a + b for a, b in zip(*parts)]
        exchange(k, [pack(sums)])

    def finish(f0, part):
        r = temporal(t2, s2, 2 + f0, part)
        rows_here = 2 * np_
        r0 = part * rows_here
        for j in range(2):
            v = xin[2 + f0 + j, pl.ds(1 + r0, rows_here)].astype(F32)
            total = v + r[:, j * C : (j + 1) * C].reshape(rows_here, cols, C)
            out[f0 + j, pl.ds(r0, rows_here)] = total.astype(BF16)

    sums = []
    for f in range(frames):
        loads[f].wait()

        def add(p, c, f=f):
            x = xin[2 + f, pl.ds(1 + 2 * p, 2)].astype(F32).reshape(-1, 8, C)
            return c[0] + jnp.sum(x, axis=0), c[1] + jnp.sum(x * x, axis=0)

        zero = jnp.zeros((8, C), F32)
        a, b = lax.fori_loop(0, pairs, add, (zero, zero))
        sums.append((jnp.sum(a, axis=0, keepdims=True), jnp.sum(b, axis=0, keepdims=True)))
    packed = [
        pack([sums[f][0], sums[f + 1][0], sums[f][1], sums[f + 1][1]]) for f in range(0, frames, 2)
    ]

    greeted = others + has_before.astype(jnp.int32) + has_after.astype(jnp.int32)
    greeted = greeted + 2 * relaying.astype(jnp.int32)
    greeted = greeted + jnp.logical_or(crossing, relayed).astype(jnp.int32)
    pl.semaphore_wait(barrier, greeted)
    send_first(0, xin)
    exchange(0, packed)
    halo0 = halo_copies(0, xin, 4, 2)
    halo5 = halo_copies(5, xin, 2, 2)
    halo1 = halo_copies(1, hid, 4, 2)
    halo2 = halo_copies(2, hid, 2, 2)
    halo3 = halo_copies(3, xin, 0, 2)
    halo4 = halo_copies(4, hid, 0, 2)
    send_halo(halo0)
    send_cross(0, xin, (0, 1))
    send_halo(halo5)
    send_cross(0, xin, (2,))

    for load in weight_loads:
        load.wait()
    gain_first = g1[...].reshape(1, C)
    gain_second = g2[...].reshape(1, C)
    pass_edges(0, xin, halo3, unrelayed)
    pass_relay(0, xin, (3,))
    whole01, whole23 = all_sums(0)
    send_rest(0, xin, whole23)
    pass_relay(0, xin, (4,))
    pair01, pair23 = pair_scales(whole01, gain_first), pair_scales(whole23, gain_first)

    activate_pair(xin, 4, pair23, halo0)
    for part in range(PARTS):
        spatial(w1, s1, 4, part)
    pass_relay(0, xin, (5,))
    activate_pair(xin, 2, pair01, halo5)
    for part in range(PARTS):
        spatial(w1, s1, 2, part)
    hidden(1, 4, [hidden_part(4, part) for part in range(PARTS)])
    send_first(1, hid)
    send_halo(halo1)
    send_cross(1, hid, (0, 1))

    pass_edges(0, xin, halo3, relayed)

    parts = []
    earlier(0, xin, w1, s1, gain_first, halo3, lambda part: parts.append(hidden_part(2, part)))
    hidden(2, 2, parts)
    send_halo(halo2)

    pass_edges(1, hid, halo4, unrelayed)
    pass_relay(1, hid, (3,))
    (whole23,) = all_sums(1)
    send_rest(1, hid, whole23)
    send_cross(1, hid, (2,))
    pass_relay(1, hid, (4,))
    activate_pair(hid, 4, pair_scales(whole23, gain_second), halo1)
    for part in range(PARTS):
        spatial(w2, s2, 4, part)
    pass_relay(1, hid, (5,))
    pass_edges(1, hid, halo4, relayed)

    (whole01,) = all_sums(2)
    activate_pair(hid, 2, pair_scales(whole01, gain_second), halo2)
    for part in range(PARTS):
        spatial(w2, s2, 2, part)
    for part in range(PARTS):
        finish(2, part)
    earlier(1, hid, w2, s2, gain_second, halo4, lambda part: finish(0, part))

    for copies in (halo0, halo1, halo2, halo5):
        wait_halo_out(copies)
    for k in range(3):
        whole = st_recv.at[k, pl.ds(0, others), pl.ds(0, sizes(k))]
        pltpu.make_async_copy(whole, whole, st_ssem.at[k]).wait()

    @pl.when(has_before)
    def _():
        for copies in (halo3, halo4):
            wait_halo_out(copies)

    @pl.when(has_after)
    def _():
        for k, buf in ((0, xin), (1, hid)):
            for piece in range(len(pieces)):
                onward(k, buf, piece).wait_send()
            onward_total(k).wait_send()

    for k, buf in ((0, xin), (1, hid)):

        @pl.when(relaying)
        def _():
            for piece in detour:
                from_relay(k, buf, piece).wait_send()


def shards(video, gain1, sp1, tp1, gain2, sp2, tp2):
    frames, rows, cols, channels = video.shape
    n_space = lax.axis_size("space")
    members = rows * n_space * cols * (channels // G)
    hbm = pl.BlockSpec(memory_space=pltpu.HBM)
    inputs = (video, gain1, sp1, tp1, gain2, sp2, tp2)
    call = pl.pallas_call(
        lambda *refs: kernel(float(members), *refs),
        out_shape=pltpu.VMEM(video.shape, BF16),
        in_specs=[hbm] * 7,
        out_specs=pl.BlockSpec(memory_space=pltpu.VMEM),
        scratch_shapes=[
            pltpu.VMEM((frames + 2, rows + 2, cols, C), BF16),
            pltpu.VMEM((frames + 2, rows // 2 + 1, 2, cols, 3 * C), BF16),
            pltpu.VMEM((frames + 2, rows // 2, 2, cols, C), BF16),
            pltpu.VMEM((frames + 2, rows // 2, 2, cols, C), BF16),
            pltpu.VMEM((frames + 2, rows + 2, cols, C), BF16),
            pltpu.VMEM((12, C, 2 * C), BF16),
            pltpu.VMEM((12, C, 2 * C), BF16),
            pltpu.VMEM((4, C, 2 * C), BF16),
            pltpu.VMEM((4, C, 2 * C), BF16),
            pltpu.VMEM((C,), F32),
            pltpu.VMEM((C,), F32),
            pltpu.VMEM((3, 8, C), F32),
            pltpu.VMEM((3, n_space - 1, 8, C), F32),
            pltpu.VMEM((2, 1, C), F32),
            pltpu.VMEM((2, 1, C), F32),
            pltpu.VMEM((2, 2, rows + 2, cols, C), BF16),
            pltpu.SemaphoreType.DMA((frames,)),
            pltpu.SemaphoreType.DMA((10,)),
            pltpu.SemaphoreType.DMA((3,)),
            pltpu.SemaphoreType.DMA((3,)),
            pltpu.SemaphoreType.DMA((6, 2)),
            pltpu.SemaphoreType.DMA((6, 2)),
            pltpu.SemaphoreType.DMA((2, 7)),
            pltpu.SemaphoreType.DMA((2, 7)),
            pltpu.SemaphoreType.DMA((2, 7)),
            pltpu.SemaphoreType.DMA((2, 7)),
        ],
        compiler_params=pltpu.CompilerParams(
            collective_id=0, has_side_effects=True, vmem_limit_bytes=62 * 2**20
        ),
        cost_estimate=pl.CostEstimate(
            flops=4 * 10**9, bytes_accessed=4 * 2**20, transcendentals=10**6
        ),
        name="block",
    )
    return call(*[pltpu.with_memory_space_constraint(x, pltpu.HBM) for x in inputs])


def solution(mesh):
    in_specs = (P("tm", "space", None, None), P(), P(), P(), P(), P(), P())
    out_specs = P("tm", "space", None, None)
    return jax.shard_map(shards, mesh=mesh, in_specs=in_specs, out_specs=out_specs, check_vma=False)
```
